256 devices in a mesh: dp: 16 (over z, core), ctx: 16 (over x, y).
Axes of the slice: x: 4, y: 4, z: 8, core: 2. Of those that a mesh axis runs over, the one named last changes fastest.
Arguments:
- queries: bfloat16 [256, 128, 576], P('dp', 'ctx'), may hold values from -60 to 60
- latent_cache: bfloat16 [16, 256, 64, 576], P('dp', 'ctx'), may hold values from -8 to 8
- w_uv: bfloat16 [128, 512, 128], P('ctx'), may hold values from -0.25 to 0.25
- w_out: bfloat16 [16384, 7168], P('ctx', 'dp'), may hold values from -0.046875 to 0.046875
- selected: int32 [256, 32], P('dp'), may hold values from 0 to 63, as said below
- row_request: int32 [256], P('dp'), may hold values from 0 to 3, as said below
- lengths: int32 [16, 4], P('dp'), may hold values from 2048 to 4096, as said below
Outputs:
- out: bfloat16 [256, 7168], P('ctx', 'dp')
The draws below stay inside these ranges and needn't reach their ends.
Inputs may be any that keep to these rules, and one draw needn't show every extreme that they name: `lengths`: each group has one request of exactly 4096 tokens and one of exactly 2048. `row_request`: every request of a group has at least one row. `selected`: a row's 32 numbers are distinct, below ceil(row_length / 64), and include the last 4 blocks of its request.
All inputs are finite; a program needn't handle non-finite values.
Results may differ from the reference program's by a relative error of at most 0.024.
Values may be sent and summed in bfloat16 or wider, within the bound.
No kernel may reach another device: no remote copies, remote signals or barrier semaphores. Data moves between devices by JAX's collectives and lax.ppermute only.
A program may use at most 128 MiB of HBM per device.

```python
import jax
import jax.numpy as jnp
from jax import lax

H = 128
DL = 512
DQK = 576
HD = 128
D = 7168
BLK = 64
TOPB = 32
RECENT = 4
REQ_BLOCKS = 64
REQ_GRP = 4
ROW_GRP = 16
POOL = 256
GROUPS = 16
ROWS = 256


def routing(base_key):
    key_list = jax.random.split(base_key, 6)
    group_perm = jax.vmap(lambda subkey: jax.random.permutation(subkey, REQ_GRP))(jax.random.split(key_list[0], GROUPS))
    base_len = jax.random.randint(key_list[1], (GROUPS, REQ_GRP), TOPB * BLK, REQ_BLOCKS * BLK + 1)
    slot_ids = jnp.arange(REQ_GRP, dtype=jnp.int32)[None, :]
    lengths = jnp.where(slot_ids == group_perm[:, 0:1], REQ_BLOCKS * BLK, jnp.where(slot_ids == group_perm[:, 1:2], TOPB * BLK, base_len)).astype(jnp.int32)
    first_rows = jax.vmap(lambda subkey: jax.random.permutation(subkey, REQ_GRP))(jax.random.split(key_list[2], GROUPS))
    extra_rows = jax.random.randint(key_list[3], (GROUPS, ROW_GRP - REQ_GRP), 0, REQ_GRP)
    row_req = jnp.concatenate([first_rows, extra_rows], axis=1).astype(jnp.int32)
    row_order = jax.vmap(lambda subkey: jax.random.permutation(subkey, ROW_GRP))(jax.random.split(key_list[4], GROUPS))
    row_req = jnp.take_along_axis(row_req, row_order, axis=1).astype(jnp.int32)
    row_len = jnp.take_along_axis(lengths, row_req, axis=1)
    block_count = (row_len + BLK - 1) // BLK
    priority = jax.vmap(lambda subkey: jax.random.permutation(subkey, REQ_BLOCKS))(jax.random.split(key_list[5], GROUPS * ROW_GRP)).reshape(GROUPS, ROW_GRP, REQ_BLOCKS).astype(jnp.int32)
    block_ids = jnp.arange(REQ_BLOCKS, dtype=jnp.int32)[None, None, :]
    priority = jnp.where(block_ids >= block_count[:, :, None] - RECENT, priority + 2 * REQ_BLOCKS, priority)
    priority = jnp.where(block_ids >= block_count[:, :, None], -1 - block_ids, priority)
    chosen = lax.top_k(priority, TOPB)[1].astype(jnp.int32)
    return (lengths, row_req.reshape(ROWS), chosen.reshape(ROWS, TOPB))


def leading_keys(base_key):
    return jnp.clip(jax.random.normal(jax.random.fold_in(base_key, 501), (GROUPS, POOL, DQK), jnp.float32), -6.0, 6.0)


def draw_lengths(key, part):
    return routing(key)[0]


def draw_row_request(key, part):
    return routing(key)[1]


def draw_selected(key, part):
    return routing(key)[2]


def draw_latent_cache(key, part):
    first_token = leading_keys(key)
    key = jax.random.fold_in(key, 11)
    key_rest = jax.random.fold_in(key, 0)
    rest_tokens = jnp.clip(jax.random.normal(key_rest, (GROUPS, POOL, BLK, DQK), jnp.float32), -6.0, 6.0)
    whole = jnp.concatenate([first_token[:, :, None, :], rest_tokens[:, :, 1:, :]], axis=2)
    return jnp.clip(whole, -8.0, 8.0).astype(jnp.bfloat16)


def draw_queries(key, part):
    key = jax.random.fold_in(key, 23)
    key_list = jax.random.split(key, 1)
    values = jnp.clip(jax.random.normal(key_list[0], (ROWS, H, DQK), jnp.float32), -6.0, 6.0)
    return values.astype(jnp.bfloat16)


def block_levels(rng, extent, shards, smallest, high):
    gain, own = 1.0, jax.random.fold_in(rng, 6)
    for dim, shards_of in shards:
        heights = jnp.exp(jax.random.uniform(jax.random.fold_in(own, dim), (shards_of,), jnp.float32, smallest / len(shards), high / len(shards)))
        gain = gain * jnp.repeat(heights, extent[dim] // shards_of).reshape([-1 if axis == dim else 1 for axis in range(len(extent))])
    return gain


def centred(rng, dims, deviation, bound, cuts=(), kind=jnp.bfloat16):
    array = jax.random.normal(rng, dims, jnp.float32) * deviation
    if len(cuts) > 0:
        array = block_levels(rng, dims, cuts, -0.22, 0.18) * array
    return jnp.clip(array, min=-bound, max=bound).astype(kind)


def setup_inputs(seed: int = 0) -> dict:
    splits = jax.random.split(jax.random.key(seed), 8)
    return {
        "queries": draw_queries(jax.random.fold_in(splits[7], 71), 0),
        "latent_cache": draw_latent_cache(jax.random.fold_in(splits[7], 71), 0),
        "w_uv": centred(splits[2], (H, DL, HD), DL ** -0.5, 0.25, ((0, 16),)),
        "w_out": centred(splits[3], (H * HD, D), (H * HD) ** -0.5, 0.046875, ((0, 16), (1, 16))),
        "selected": draw_selected(jax.random.fold_in(splits[7], 71), 0),
        "row_request": draw_row_request(jax.random.fold_in(splits[7], 71), 0),
        "lengths": draw_lengths(jax.random.fold_in(splits[7], 71), 0),
    }


softmax_scale = 192.0 ** -0.5
masked_score = -1.0e30


def group_hidden(packed, w_uv):
    group_queries, group_cache, group_selected, group_request, group_lengths = packed
    row_length = group_lengths[group_request.astype(jnp.int32)]
    blocks = (group_request[:, None] * REQ_BLOCKS + group_selected).astype(jnp.int32)
    picked = group_cache[blocks].reshape(ROW_GRP, TOPB * BLK, DQK)
    position = (group_selected[:, :, None] * BLK + jnp.arange(BLK, dtype=jnp.int32)[None, None, :]).reshape(ROW_GRP, TOPB * BLK)
    valid_tokens = position < row_length[:, None]
    scores = softmax_scale * jnp.einsum("rhc,rtc->rht", group_queries.astype(jnp.float32), picked.astype(jnp.float32))
    masked_scores = jnp.where(valid_tokens[:, None, :], scores, masked_score)
    row_peak = jnp.max(masked_scores, axis=2, keepdims=True)
    softmax_num = jnp.where(valid_tokens[:, None, :], jnp.exp(masked_scores - row_peak), 0.0)
    denominator = jnp.sum(softmax_num, axis=2)
    weights = lax.optimization_barrier(softmax_num.astype(jnp.bfloat16))
    numerator = jnp.einsum("rht,rtc->rhc", weights.astype(jnp.float32), picked[:, :, :DL].astype(jnp.float32))
    latent = lax.optimization_barrier((numerator / denominator[:, :, None]).astype(jnp.bfloat16))
    hidden = jnp.einsum("rhl,hlv->rhv", latent.astype(jnp.float32), w_uv.astype(jnp.float32)).astype(jnp.bfloat16)
    return hidden.reshape(ROW_GRP, H * HD)


def reference(queries, latent_cache, w_uv, w_out, selected, row_request, lengths):
    packed = (queries.reshape(GROUPS, ROW_GRP, H, DQK), latent_cache, selected.reshape(GROUPS, ROW_GRP, TOPB), row_request.reshape(GROUPS, ROW_GRP), lengths)
    hidden = lax.map(lambda packed_group: group_hidden(packed_group, w_uv), packed)
    flat_hidden = hidden.reshape(ROWS, H * HD)
    return jnp.dot(flat_hidden, w_out, preferred_element_type=jnp.float32).astype(jnp.bfloat16)
```

```python
import functools

import jax
import jax.numpy as jnp
from jax import lax
from jax.experimental import pallas as pl
from jax.experimental.pallas import tpu as pltpu
from jax.sharding import PartitionSpec as P

REQ_BLOCKS = 64
ROWS = 16
REQS = 4
SLOTS = 13
HEADS = 8
CTX = 16
LATENT = 512
ROPE = 64
NOPE_ROWS = SLOTS * HEADS
SEND_ROWS = 120
BACK_ROWS = 112
FLOOR = -30000.0
MASKED = -1e30
LO, HI = 64, 32

VMEM = pl.BlockSpec(memory_space=pltpu.VMEM)
SMEM = pl.BlockSpec(memory_space=pltpu.SMEM)


def pack_kernel(request_ref, queries_ref, out_ref, nope, rope, count):
    rope[...] = jnp.zeros_like(rope)
    for x in range(REQS):
        count[x] = 0
    for r in range(ROWS):
        x = request_ref[r]
        s = count[x]
        count[x] = s + 1
        q = queries_ref[r].astype(jnp.float32)
        nope[x, pl.ds(pl.multiple_of(s * HEADS, HEADS), HEADS), :] = q[:, :LATENT]
        part = q[:, LATENT:]
        none = jnp.zeros_like(part)
        odd = s % 2 == 1
        pair = jnp.where(
            odd, jnp.concatenate([none, part], axis=1), jnp.concatenate([part, none], axis=1)
        )
        top = pl.ds(pl.multiple_of(s // 8 * HEADS, HEADS), HEADS)
        lanes = pl.ds(pl.multiple_of(s % 8 // 2 * 128, 128), 128)
        rope[x, top, lanes] = rope[x, top, lanes] + pair
    for x in range(REQS):
        full = jnp.concatenate([nope[x], rope[x]], axis=0).astype(jnp.bfloat16)
        for y in range(CTX // REQS):
            out_ref[x * (CTX // REQS) + y] = full


def attend_kernel(
    place_ref, request_ref, lengths_ref, selected_ref, recv_ref, cache_ref, out_ref,
    bias, rope_keys, extra, row_of,
):
    tokens = cache_ref.shape[0]
    x, y = place_ref[0], place_ref[1]
    for s in range(SLOTS + 1):
        row_of[s] = 0
    count = jnp.int32(0)
    for r in range(ROWS):
        mine = request_ref[r] == x
        row_of[jnp.where(mine, count, SLOTS + 1)] = r
        count = count + mine.astype(jnp.int32)

    token = lax.broadcasted_iota(jnp.int32, (ROWS, tokens), 1) + y * tokens
    block = token // (tokens // 16)
    chosen = selected_ref[:, 0:1] == block
    for k in range(1, selected_ref.shape[1]):
        chosen = chosen | (selected_ref[:, k : k + 1] == block)
    bias[...] = jnp.where(chosen & (token < lengths_ref[x]), 0.0, MASKED)

    tail = cache_ref[:, LATENT:]
    rope_keys[...] = jnp.concatenate([tail, tail], axis=1)
    lane = lax.broadcasted_iota(jnp.int32, (CTX, HEADS, 128), 2)
    extra[...] = jnp.where(lane < HI, FLOOR, 0.0)
    half = lax.broadcasted_iota(jnp.int32, (CTX, HEADS, 128), 2) < ROPE
    contract = (((1,), (1,)), ((), ()))

    def pair_step(p, carry):
        rows = pl.ds(pl.multiple_of(p * 2 * HEADS, 2 * HEADS), 2 * HEADS)
        q = recv_ref[:, rows, :].reshape(CTX * 2 * HEADS, LATENT)
        lanes = pl.ds(pl.multiple_of(p % 4 * 128, 128), 128)
        both = recv_ref[:, NOPE_ROWS - 8 : SEND_ROWS, lanes].astype(jnp.float32)
        part = jnp.where(p < 4, both[:, 8:16], both[:, 16:24])
        zero = jnp.zeros_like(part)
        qr = jnp.stack([jnp.where(half, part, zero), jnp.where(half, zero, part)], axis=1)
        qr = qr.reshape(CTX * 2 * HEADS, 128).astype(jnp.bfloat16)
        scores = lax.dot_general(
            q, cache_ref[:, :LATENT], contract, preferred_element_type=jnp.float32
        ) + lax.dot_general(qr, rope_keys[...], contract, preferred_element_type=jnp.float32)
        scores = scores.reshape(CTX, 2, HEADS, tokens) * (192.0**-0.5)
        bias_a = bias[pl.ds(row_of[2 * p], 1), :]
        bias_b = bias[pl.ds(row_of[2 * p + 1], 1), :]
        scores = scores + jnp.stack([bias_a, bias_b], axis=0)[None]
        peak = jnp.maximum(jnp.max(scores, axis=3, keepdims=True), FLOOR)
        peak = peak.astype(jnp.bfloat16).astype(jnp.float32)
        probs = jnp.exp(scores - peak)
        total = jnp.sum(probs, axis=3, keepdims=True)
        weights = probs.reshape(CTX * 2 * HEADS, tokens).astype(jnp.bfloat16)
        numerator = jnp.dot(weights, cache_ref[:, :LATENT], preferred_element_type=jnp.float32)
        out_ref[:, rows, :] = numerator.astype(jnp.bfloat16).reshape(CTX, 2 * HEADS, LATENT)
        high = total.astype(jnp.bfloat16).astype(jnp.float32)
        low = total - high
        held = extra[...]
        for j in range(2):
            s = 2 * p + j
            held = jnp.where(lane == s, peak[:, j], held)
            held = jnp.where(lane == s + HI, high[:, j], held)
            held = jnp.where(lane == s + LO, low[:, j], held)
        extra[...] = held
        return carry

    lax.fori_loop(0, (count + 1) // 2, pair_step, 0)
    last = out_ref[:, BACK_ROWS - 16 :, :128].astype(jnp.float32)
    last = jnp.concatenate([last[:, :8], extra[...]], axis=1)
    out_ref[:, BACK_ROWS - 16 :, :128] = last.astype(jnp.bfloat16)


def combine_kernel(request_ref, recv_ref, w_uv_ref, out_ref, share, latent, count):
    span = CTX // REQS
    for x in range(REQS):
        count[x] = 0
        parts = [
            recv_ref[x * span + y, BACK_ROWS - 16 :, :128].astype(jnp.float32)[8:]
            for y in range(span)
        ]
        peak = functools.reduce(jnp.maximum, parts)
        scale = [jnp.exp(part - peak) for part in parts]
        total = sum(
            f * (jnp.roll(part, -HI, axis=1) + jnp.roll(part, -LO, axis=1))
            for f, part in zip(scale, parts)
        )
        for y in range(span):
            share[x * span + y] = scale[y] / total
    lane = lax.broadcasted_iota(jnp.int32, (HEADS, 128), 1)
    for r in range(ROWS):
        x = request_ref[r]
        s = count[x]
        count[x] = s + 1
        rows = pl.ds(pl.multiple_of(s // 2 * 16, 16), 16)
        value = None
        for y in range(span):
            both = recv_ref[x * span + y, rows, :].astype(jnp.float32)
            part = jnp.where(s % 2 == 1, both[8:], both[:8])
            factor = jnp.sum(
                jnp.where(lane == s, share[x * span + y], 0.0), axis=1, keepdims=True
            )
            value = factor * part if value is None else value + factor * part
        latent[r] = value
    width = w_uv_ref.shape[2]
    for h in range(HEADS):
        hidden = jnp.dot(
            latent[:, h, :].astype(jnp.bfloat16), w_uv_ref[h], preferred_element_type=jnp.float32
        )
        out_ref[:, h * width : (h + 1) * width] = hidden.astype(jnp.bfloat16)


def on_device(queries, latent_cache, w_uv, w_out, selected, row_request, lengths):
    params = pltpu.CompilerParams(vmem_limit_bytes=48 * 1024 * 1024)
    place = lax.axis_index("ctx")
    place = jnp.stack([place // REQS, place % REQS]).astype(jnp.int32)
    sent = pl.pallas_call(
        pack_kernel,
        out_shape=jax.ShapeDtypeStruct((CTX, SEND_ROWS, LATENT), jnp.bfloat16),
        in_specs=[SMEM, VMEM],
        out_specs=VMEM,
        scratch_shapes=[
            pltpu.VMEM((REQS, NOPE_ROWS, LATENT), jnp.float32),
            pltpu.VMEM((REQS, 2 * HEADS, LATENT), jnp.float32),
            pltpu.SMEM((REQS,), jnp.int32),
        ],
        compiler_params=params,
    )(row_request, queries)
    recv = lax.all_to_all(sent, "ctx", 0, 0)
    keys = latent_cache.reshape(-1, latent_cache.shape[3])
    back = pl.pallas_call(
        attend_kernel,
        out_shape=jax.ShapeDtypeStruct((CTX, BACK_ROWS, LATENT), jnp.bfloat16),
        in_specs=[SMEM, SMEM, SMEM, VMEM, VMEM, VMEM],
        out_specs=VMEM,
        scratch_shapes=[
            pltpu.VMEM((ROWS, keys.shape[0]), jnp.float32),
            pltpu.VMEM((keys.shape[0], 2 * ROPE), jnp.bfloat16),
            pltpu.VMEM((CTX, HEADS, 128), jnp.float32),
            pltpu.SMEM((SLOTS + 2,), jnp.int32),
        ],
        compiler_params=params,
    )(place, row_request, lengths[0], selected, recv, keys)
    recv = lax.all_to_all(back, "ctx", 0, 0)
    hidden = pl.pallas_call(
        combine_kernel,
        out_shape=jax.ShapeDtypeStruct((ROWS, HEADS * w_uv.shape[2]), jnp.bfloat16),
        in_specs=[SMEM, VMEM, VMEM],
        out_specs=VMEM,
        scratch_shapes=[
            pltpu.VMEM((CTX, HEADS, 128), jnp.float32),
            pltpu.VMEM((ROWS, HEADS, LATENT), jnp.float32),
            pltpu.SMEM((REQS,), jnp.int32),
        ],
        compiler_params=params,
    )(row_request, recv, w_uv)
    hidden = lax.all_gather(hidden, "dp", axis=0, tiled=True)
    partial_out = jnp.dot(hidden, w_out, preferred_element_type=jnp.float32)
    partial_out = partial_out.astype(jnp.bfloat16).reshape(CTX, -1, w_out.shape[1])
    parts = lax.all_to_all(partial_out, "ctx", 0, 0)
    return jnp.sum(parts.astype(jnp.float32), axis=0).astype(jnp.bfloat16)


def solution(mesh):
    in_specs = (
        P("dp", "ctx", None),
        P("dp", "ctx", None, None),
        P("ctx", None, None),
        P("ctx", "dp"),
        P("dp", None),
        P("dp"),
        P("dp", None),
    )
    out_specs = P("ctx", "dp")
    return jax.shard_map(
        on_device, mesh=mesh, in_specs=in_specs, out_specs=out_specs, check_vma=False
    )
```

```python
import functools

import jax
import jax.numpy as jnp
from jax import lax
from jax.experimental import pallas as pl
from jax.experimental.pallas import tpu as pltpu
from jax.sharding import PartitionSpec as P

REQ_BLOCKS = 64
ROWS = 16
REQS = 4
SLOTS = (6, 7, 8, 10, 13)
HEADS = 8
CTX = 16
LATENT = 512
ROPE = 64
FLOOR = -30000.0
MASKED = -1e30
LO, HI = 64, 32


def send_rows(slots):
    return slots * HEADS + -(-slots // 8) * HEADS


def back_rows(slots):
    return slots * HEADS + HEADS


def tail_start(slots):
    return slots * HEADS // 16 * 16


VMEM = pl.BlockSpec(memory_space=pltpu.VMEM)
SMEM = pl.BlockSpec(memory_space=pltpu.SMEM)


def pack_kernel(request_ref, queries_ref, out_ref, nope, rope, count):
    rope[...] = jnp.zeros_like(rope)
    for x in range(REQS):
        count[x] = 0
    for r in range(ROWS):
        x = request_ref[r]
        s = count[x]
        count[x] = s + 1
        q = queries_ref[r].astype(jnp.float32)
        nope[x, pl.ds(pl.multiple_of(s * HEADS, HEADS), HEADS), :] = q[:, :LATENT]
        part = q[:, LATENT:]
        none = jnp.zeros_like(part)
        odd = s % 2 == 1
        pair = jnp.where(
            odd, jnp.concatenate([none, part], axis=1), jnp.concatenate([part, none], axis=1)
        )
        top = pl.ds(pl.multiple_of(s // 8 * HEADS, HEADS), HEADS)
        lanes = pl.ds(pl.multiple_of(s % 8 // 2 * 128, 128), 128)
        rope[x, top, lanes] = rope[x, top, lanes] + pair
    for x in range(REQS):
        full = jnp.concatenate([nope[x], rope[x]], axis=0).astype(jnp.bfloat16)
        for y in range(CTX // REQS):
            out_ref[x * (CTX // REQS) + y] = full


def attend_kernel(
    slots, place_ref, request_ref, lengths_ref, selected_ref, recv_ref, cache_ref, out_ref,
    bias, rope_keys, extra, row_of,
):
    tokens = cache_ref.shape[0]
    x, y = place_ref[0], place_ref[1]
    for s in range(slots + 1):
        row_of[s] = 0
    count = jnp.int32(0)
    for r in range(ROWS):
        mine = request_ref[r] == x
        row_of[jnp.where(mine, count, slots + 1)] = r
        count = count + mine.astype(jnp.int32)

    token = lax.broadcasted_iota(jnp.int32, (ROWS, tokens), 1) + y * tokens
    block = token // (tokens // 16)
    chosen = selected_ref[:, 0:1] == block
    for k in range(1, selected_ref.shape[1]):
        chosen = chosen | (selected_ref[:, k : k + 1] == block)
    bias[...] = jnp.where(chosen & (token < lengths_ref[x]), 0.0, MASKED)

    tail = cache_ref[:, LATENT:]
    rope_keys[...] = jnp.concatenate([tail, tail], axis=1)
    lane = lax.broadcasted_iota(jnp.int32, (CTX, HEADS, 128), 2)
    extra[...] = jnp.where(lane < HI, FLOOR, 0.0)
    half = lax.broadcasted_iota(jnp.int32, (CTX, HEADS, 128), 2) < ROPE
    contract = (((1,), (1,)), ((), ()))

    def pair_step(p, carry):
        rows = pl.ds(pl.multiple_of(p * 2 * HEADS, 2 * HEADS), 2 * HEADS)
        q = recv_ref[:, rows, :].reshape(CTX * 2 * HEADS, LATENT)
        lanes = pl.ds(pl.multiple_of(p % 4 * 128, 128), 128)
        both = recv_ref[:, tail_start(slots) :, lanes].astype(jnp.float32)
        skip = slots * HEADS - tail_start(slots)
        part = both[:, skip : skip + HEADS]
        if slots > 8:
            part = jnp.where(p < 4, part, both[:, skip + HEADS : skip + 2 * HEADS])
        zero = jnp.zeros_like(part)
        qr = jnp.stack([jnp.where(half, part, zero), jnp.where(half, zero, part)], axis=1)
        qr = qr.reshape(CTX * 2 * HEADS, 128).astype(jnp.bfloat16)
        scores = lax.dot_general(
            q, cache_ref[:, :LATENT], contract, preferred_element_type=jnp.float32
        ) + lax.dot_general(qr, rope_keys[...], contract, preferred_element_type=jnp.float32)
        scores = scores.reshape(CTX, 2, HEADS, tokens) * (192.0**-0.5)
        bias_a = bias[pl.ds(row_of[2 * p], 1), :]
        bias_b = bias[pl.ds(row_of[2 * p + 1], 1), :]
        scores = scores + jnp.stack([bias_a, bias_b], axis=0)[None]
        peak = jnp.maximum(jnp.max(scores, axis=3, keepdims=True), FLOOR)
        peak = peak.astype(jnp.bfloat16).astype(jnp.float32)
        probs = jnp.exp(scores - peak)
        total = jnp.sum(probs, axis=3, keepdims=True)
        weights = probs.reshape(CTX * 2 * HEADS, tokens).astype(jnp.bfloat16)
        numerator = jnp.dot(weights, cache_ref[:, :LATENT], preferred_element_type=jnp.float32)
        out_ref[:, rows, :] = numerator.astype(jnp.bfloat16).reshape(CTX, 2 * HEADS, LATENT)
        high = total.astype(jnp.bfloat16).astype(jnp.float32)
        low = total - high
        held = extra[...]
        for j in range(2):
            s = 2 * p + j
            held = jnp.where(lane == s, peak[:, j], held)
            held = jnp.where(lane == s + HI, high[:, j], held)
            held = jnp.where(lane == s + LO, low[:, j], held)
        extra[...] = held
        return carry

    lax.fori_loop(0, (count + 1) // 2, pair_step, 0)
    last = extra[...]
    if slots % 2 == 1:
        kept = out_ref[:, tail_start(slots) :, :128].astype(jnp.float32)
        last = jnp.concatenate([kept[:, :HEADS], last], axis=1)
    out_ref[:, tail_start(slots) :, :128] = last.astype(jnp.bfloat16)


def combine_kernel(slots, request_ref, recv_ref, w_uv_ref, out_ref, share, latent, count):
    span = CTX // REQS
    for x in range(REQS):
        count[x] = 0
        parts = [
            recv_ref[x * span + y, tail_start(slots) :, :128].astype(jnp.float32)[-HEADS:]
            for y in range(span)
        ]
        peak = functools.reduce(jnp.maximum, parts)
        scale = [jnp.exp(part - peak) for part in parts]
        total = sum(
            f * (jnp.roll(part, -HI, axis=1) + jnp.roll(part, -LO, axis=1))
            for f, part in zip(scale, parts)
        )
        for y in range(span):
            share[x * span + y] = scale[y] / total
    lane = lax.broadcasted_iota(jnp.int32, (HEADS, 128), 1)
    for r in range(ROWS):
        x = request_ref[r]
        s = count[x]
        count[x] = s + 1
        rows = pl.ds(pl.multiple_of(s // 2 * 16, 16), 16)
        value = None
        for y in range(span):
            both = recv_ref[x * span + y, rows, :].astype(jnp.float32)
            part = jnp.where(s % 2 == 1, both[8:], both[:8])
            factor = jnp.sum(
                jnp.where(lane == s, share[x * span + y], 0.0), axis=1, keepdims=True
            )
            value = factor * part if value is None else value + factor * part
        latent[r] = value
    width = w_uv_ref.shape[2]
    for h in range(HEADS):
        hidden = jnp.dot(
            latent[:, h, :].astype(jnp.bfloat16), w_uv_ref[h], preferred_element_type=jnp.float32
        )
        out_ref[:, h * width : (h + 1) * width] = hidden.astype(jnp.bfloat16)


def group_hidden(slots, queries, keys, w_uv, selected, row_request, lengths, place):
    params = pltpu.CompilerParams(vmem_limit_bytes=40 * 1024 * 1024)
    sent = pl.pallas_call(
        pack_kernel,
        out_shape=jax.ShapeDtypeStruct((CTX, send_rows(slots), LATENT), jnp.bfloat16),
        in_specs=[SMEM, VMEM],
        out_specs=VMEM,
        scratch_shapes=[
            pltpu.VMEM((REQS, slots * HEADS, LATENT), jnp.float32),
            pltpu.VMEM((REQS, send_rows(slots) - slots * HEADS, LATENT), jnp.float32),
            pltpu.SMEM((REQS,), jnp.int32),
        ],
        compiler_params=params,
    )(row_request, queries)
    recv = lax.all_to_all(sent, "ctx", 0, 0)
    back = pl.pallas_call(
        functools.partial(attend_kernel, slots),
        out_shape=jax.ShapeDtypeStruct((CTX, back_rows(slots), LATENT), jnp.bfloat16),
        in_specs=[SMEM, SMEM, SMEM, VMEM, VMEM, VMEM],
        out_specs=VMEM,
        scratch_shapes=[
            pltpu.VMEM((ROWS, keys.shape[0]), jnp.float32),
            pltpu.VMEM((keys.shape[0], 2 * ROPE), jnp.bfloat16),
            pltpu.VMEM((CTX, HEADS, 128), jnp.float32),
            pltpu.SMEM((slots + 2,), jnp.int32),
        ],
        compiler_params=params,
    )(place, row_request, lengths, selected, recv, keys)
    recv = lax.all_to_all(back, "ctx", 0, 0)
    return pl.pallas_call(
        functools.partial(combine_kernel, slots),
        out_shape=jax.ShapeDtypeStruct((ROWS, HEADS * w_uv.shape[2]), jnp.bfloat16),
        in_specs=[SMEM, VMEM, VMEM],
        out_specs=VMEM,
        scratch_shapes=[
            pltpu.VMEM((CTX, HEADS, 128), jnp.float32),
            pltpu.VMEM((ROWS, HEADS, LATENT), jnp.float32),
            pltpu.SMEM((REQS,), jnp.int32),
        ],
        compiler_params=params,
    )(row_request, recv, w_uv)


def on_device(queries, latent_cache, w_uv, w_out, selected, row_request, lengths):
    place = lax.axis_index("ctx")
    place = jnp.stack([place // REQS, place % REQS]).astype(jnp.int32)
    counts = jnp.sum(row_request[:, None] == jnp.arange(REQS, dtype=jnp.int32)[None], axis=0)
    needed = jnp.max(counts)
    branch = sum((needed > slots).astype(jnp.int32) for slots in SLOTS[:-1])
    keys = latent_cache.reshape(-1, latent_cache.shape[3])
    hidden = lax.switch(
        branch,
        [functools.partial(group_hidden, slots) for slots in SLOTS],
        queries, keys, w_uv, selected, row_request, lengths[0], place,
    )
    hidden = lax.all_gather(hidden, "dp", axis=0, tiled=True)
    partial_out = jnp.dot(hidden, w_out, preferred_element_type=jnp.float32)
    partial_out = partial_out.astype(jnp.bfloat16).reshape(CTX, -1, w_out.shape[1])
    parts = lax.all_to_all(partial_out, "ctx", 0, 0)
    return jnp.sum(parts.astype(jnp.float32), axis=0).astype(jnp.bfloat16)


def solution(mesh):
    in_specs = (
        P("dp", "ctx", None),
        P("dp", "ctx", None, None),
        P("ctx", None, None),
        P("ctx", "dp"),
        P("dp", None),
        P("dp"),
        P("dp", None),
    )
    out_specs = P("ctx", "dp")
    return jax.shard_map(
        on_device, mesh=mesh, in_specs=in_specs, out_specs=out_specs, check_vma=False
    )
```

```python
import functools

import jax
import jax.numpy as jnp
from jax import lax
from jax.experimental import pallas as pl
from jax.experimental.pallas import tpu as pltpu
from jax.sharding import PartitionSpec as P

REQ_BLOCKS = 64
ROWS = 16
REQS = 4
SLOTS = (7, 8, 10, 14)
HEADS = 8
HALF = 4
CTX = 16
SPAN = CTX // REQS
LATENT = 512
ROPE = 64
FLOOR = -300000.0
SCALE = 192.0**-0.5 * 1.4426950408889634
MASKED = -1e30
LO, HI = 64, 32

VMEM = pl.BlockSpec(memory_space=pltpu.VMEM)
SMEM = pl.BlockSpec(memory_space=pltpu.SMEM)


def message_rows(slots):
    return -(-(slots + 1) // 2) * 8 if slots < 8 else slots * HALF + 8


def partner(y, core):
    return jnp.where(core == 0, y ^ 1, (y + 1 - 2 * (1 - y % 2)) % SPAN)


def upper(shape, axis):
    return lax.broadcasted_iota(jnp.int32, shape, axis) < HALF


def plan_kernel(request_ref, out_ref, count):
    for x in range(REQS):
        count[x] = 0
    for r in range(ROWS):
        x = request_ref[r]
        count[x] = count[x] + 1
    needed = functools.reduce(jnp.maximum, [count[x] for x in range(REQS)])
    out_ref[0] = sum((needed > slots).astype(jnp.int32) for slots in SLOTS[:-1])


def pack_kernel(
    slots, ctx_ref, dp_ref, request_ref, lengths_ref, selected_ref, queries_ref, out_ref,
    bias_ref, nope, rope, count,
):
    rope[...] = jnp.zeros_like(rope)
    for x in range(REQS):
        count[x] = 0
    for r in range(ROWS):
        x = request_ref[r]
        s = count[x]
        count[x] = s + 1
        q = queries_ref[r].astype(jnp.float32)
        moved = pltpu.roll(q, HALF, 0)
        tile = pl.ds(pl.multiple_of(s // 2 * 8, 8), 8)
        lanes = pl.ds(pl.multiple_of(s % 8 // 2 * 128, 128), 128)
        first = upper((8, LATENT), 0) == (s % 2 == 0)
        spot = lax.broadcasted_iota(jnp.int32, (8, 128), 1) < ROPE
        spot = (spot == (s % 2 == 0)) & (upper((8, 128), 0) == (s < 8))
        for h in range(2):
            value = jnp.where(s % 2 == h, q[:, :LATENT], moved[:, :LATENT])
            nope[x, h, tile, :] = jnp.where(first, value, nope[x, h, tile, :])
            part = jnp.where(s // 8 == h, q[:, LATENT:], moved[:, LATENT:])
            part = jnp.concatenate([part, part], axis=1)
            rope[x, h, :, lanes] = rope[x, h, :, lanes] + jnp.where(spot, part, 0.0)
    for x in range(REQS):
        for h in range(2):
            if slots % 2 == 1:
                last = jnp.where(
                    upper((8, LATENT), 0), nope[x, h, -8:, :], pltpu.roll(rope[x, h], HALF, 0)
                )
                full = jnp.concatenate([nope[x, h, :-8, :], last], axis=0)
            else:
                full = jnp.concatenate([nope[x, h], rope[x, h]], axis=0)
            full = full.astype(jnp.bfloat16)
            for y in range(h, SPAN, 2):
                out_ref[x * SPAN + y] = full
    x, y = ctx_ref[0] // SPAN, ctx_ref[0] % SPAN
    places = (y, partner(y, dp_ref[0] % 2))
    tokens = bias_ref.shape[2]
    for i in range(2):
        token = lax.broadcasted_iota(jnp.int32, (ROWS, tokens), 1) + places[i] * tokens
        block = token // (tokens // 16)
        chosen = selected_ref[:, 0:1] == block
        for k in range(1, selected_ref.shape[1]):
            chosen = chosen | (selected_ref[:, k : k + 1] == block)
        bias_ref[i] = jnp.where(chosen & (token < lengths_ref[x]), 0.0, MASKED)


def attend_kernel(
    slots, ctx_ref, request_ref, recv_ref, bias, own_ref, other_ref, out_ref, rope_keys, extra,
    row_of,
):
    tokens = own_ref.shape[0]
    x = ctx_ref[0] // SPAN
    keys = (own_ref, other_ref)
    for s in range(16):
        row_of[s] = 0
    count = jnp.int32(0)
    for r in range(ROWS):
        mine = request_ref[r] == x
        row_of[jnp.where(mine, count, 16)] = r
        count = count + mine.astype(jnp.int32)

    for i in range(2):
        tail = keys[i][:, LATENT:]
        rope_keys[i] = jnp.concatenate([tail, tail], axis=1)
    lane = lax.broadcasted_iota(jnp.int32, (CTX, 8, 128), 2)
    extra[...] = jnp.where(lane < HI, FLOOR, 0.0)
    top = upper((CTX, 8, 128), 1)
    spot = (lane < ROPE) == top
    contract = (((1,), (1,)), ((), ()))
    rope_start = slots * HALF // 8 * 8

    def quad_step(p, carry):
        rows = pl.ds(pl.multiple_of(p * 16, 16), 16)
        q = recv_ref[:, rows, :].reshape(CTX * 16, LATENT)
        parts = []
        for u in range(2):
            lanes = pl.ds(pl.multiple_of(p % 2 * 256 + u * 128, 128), 128)
            part = recv_ref[:, rope_start // 16 * 16 : rope_start + 8, lanes].astype(jnp.float32)
            part = part[:, -8:]
            moved = pltpu.roll(part, HALF, 1)
            low = (slots % 2 == 1) | (p >= 2)
            part = jnp.where(low == top, moved, part)
            parts.append(jnp.where(spot, part, 0.0))
        qr = jnp.stack(parts, axis=1).reshape(CTX * 16, 128).astype(jnp.bfloat16)
        wide = upper((8, tokens), 0)
        scores = []
        for i in range(2):
            score = lax.dot_general(
                q, keys[i][:, :LATENT], contract, preferred_element_type=jnp.float32
            ) + lax.dot_general(qr, rope_keys[i], contract, preferred_element_type=jnp.float32)
            add = [bias[i, pl.ds(row_of[4 * p + j], 1), :] for j in range(4)]
            add = [jnp.where(wide, add[2 * u], add[2 * u + 1]) for u in range(2)]
            scores.append(score.reshape(CTX, 2, 8, tokens) + jnp.stack(add, axis=0)[None])
        peak = [jnp.max(score, axis=3, keepdims=True) for score in scores]
        peak = jnp.maximum(jnp.maximum(peak[0], peak[1]), FLOOR)
        peak = peak.astype(jnp.bfloat16).astype(jnp.float32)
        probs = [jnp.exp2((score - peak) * SCALE) for score in scores]
        total = sum(jnp.sum(prob, axis=3, keepdims=True) for prob in probs)
        numerator = sum(
            jnp.dot(
                probs[i].reshape(CTX * 16, tokens).astype(jnp.bfloat16),
                keys[i][:, :LATENT],
                preferred_element_type=jnp.float32,
            )
            for i in range(2)
        )
        out_ref[:, rows, :] = numerator.astype(jnp.bfloat16).reshape(CTX, 16, LATENT)
        high = total.astype(jnp.bfloat16).astype(jnp.float32)
        low = total - high
        held = extra[...]
        for u in range(2):
            s = 2 * p + u
            held = jnp.where(lane == s, peak[:, u], held)
            held = jnp.where(lane == s + HI, high[:, u], held)
            held = jnp.where(lane == s + LO, low[:, u], held)
        extra[...] = held
        return carry

    lax.fori_loop(0, (count + 3) // 4, quad_step, 0)
    start = rope_start // 16 * 16
    last = extra[...]
    last = jnp.concatenate([last, pltpu.roll(last, HALF, 1)], axis=2)
    if slots % 2 == 1:
        last = pltpu.roll(last, HALF, 1)
        kept = out_ref[:, start:, :256].astype(jnp.float32)
        last = jnp.concatenate(
            [kept[:, :-8], jnp.where(upper((CTX, 8, 256), 1), kept[:, -8:], last)], axis=1
        )
    elif start < rope_start:
        kept = out_ref[:, start:, :256].astype(jnp.float32)
        last = jnp.concatenate([kept[:, :-8], last], axis=1)
    out_ref[:, start:, :256] = last.astype(jnp.bfloat16)


def combine_kernel(slots, request_ref, recv_ref, w_uv_ref, out_ref, share, latent, count):
    start = slots * HALF // 16 * 16
    top = upper((8, 128), 0)
    for x in range(REQS):
        count[x] = 0
        for h in range(2):
            parts = []
            for y in range(h, SPAN, 2):
                part = recv_ref[x * SPAN + y, start:, :256].astype(jnp.float32)[-8:]
                if slots % 2 == 1:
                    part = pltpu.roll(part, HALF, 0)
                parts.append(
                    jnp.where(top, part[:, :128], pltpu.roll(part[:, 128:], HALF, 0))
                )
            peak = jnp.maximum(parts[0], parts[1])
            scale = [jnp.exp2((part - peak) * SCALE) for part in parts]
            total = sum(
                f * (pltpu.roll(part, 128 - HI, 1) + pltpu.roll(part, 128 - LO, 1))
                for f, part in zip(scale, parts)
            )
            for i in range(2):
                share[x * SPAN + h + 2 * i] = scale[i] / total
    lane = lax.broadcasted_iota(jnp.int32, (8, 128), 1)
    wide = upper((8, LATENT), 0)
    for r in range(ROWS):
        x = request_ref[r]
        s = count[x]
        count[x] = s + 1
        rows = pl.ds(pl.multiple_of(s // 4 * 16, 16), 16)
        values = []
        for h in range(2):
            value = 0.0
            for y in range(h, SPAN, 2):
                both = recv_ref[x * SPAN + y, rows, :].astype(jnp.float32)
                part = jnp.where(s % 4 >= 2, both[8:], both[:8])
                factor = jnp.sum(
                    jnp.where(lane == s // 2, share[x * SPAN + y], 0.0), axis=1, keepdims=True
                )
                value = value + factor * part
            values.append(jnp.where(s % 2 == h, value, pltpu.roll(value, HALF, 0)))
        latent[r] = jnp.where(wide, values[0], values[1])
    width = w_uv_ref.shape[2]
    for h in range(HEADS):
        hidden = jnp.dot(
            latent[:, h, :].astype(jnp.bfloat16), w_uv_ref[h], preferred_element_type=jnp.float32
        )
        out_ref[:, h * width : (h + 1) * width] = hidden.astype(jnp.bfloat16)


PARAMS = pltpu.CompilerParams(vmem_limit_bytes=40 * 1024 * 1024)


def to_keys(slots, queries, selected, row_request, lengths, ctx, dp, tokens):
    sent, bias = pl.pallas_call(
        functools.partial(pack_kernel, slots),
        out_shape=(
            jax.ShapeDtypeStruct((CTX, message_rows(slots), LATENT), jnp.bfloat16),
            jax.ShapeDtypeStruct((2, ROWS, tokens), jnp.float32),
        ),
        in_specs=[SMEM, SMEM, SMEM, SMEM, VMEM, VMEM],
        out_specs=(VMEM, VMEM),
        scratch_shapes=[
            pltpu.VMEM((REQS, 2, -(-slots // 2) * 8, LATENT), jnp.float32),
            pltpu.VMEM((REQS, 2, 8, LATENT), jnp.float32),
            pltpu.SMEM((REQS,), jnp.int32),
        ],
        compiler_params=PARAMS,
    )(ctx, dp, row_request, lengths, selected, queries)
    recv = lax.all_to_all(sent, "ctx", 0, 0)
    spare = message_rows(SLOTS[-1]) - recv.shape[1]
    return jnp.pad(recv, ((0, 0), (0, spare), (0, 0))), bias


def to_heads(slots, recv, bias, keys, other_keys, w_uv, row_request, ctx):
    back = pl.pallas_call(
        functools.partial(attend_kernel, slots),
        out_shape=jax.ShapeDtypeStruct((CTX, message_rows(slots), LATENT), jnp.bfloat16),
        in_specs=[SMEM, SMEM, VMEM, VMEM, VMEM, VMEM],
        out_specs=VMEM,
        scratch_shapes=[
            pltpu.VMEM((2, keys.shape[0], 2 * ROPE), jnp.bfloat16),
            pltpu.VMEM((CTX, 8, 128), jnp.float32),
            pltpu.SMEM((17,), jnp.int32),
        ],
        compiler_params=PARAMS,
    )(ctx, row_request, recv, bias, keys, other_keys)
    recv = lax.all_to_all(back, "ctx", 0, 0)
    return pl.pallas_call(
        functools.partial(combine_kernel, slots),
        out_shape=jax.ShapeDtypeStruct((ROWS, HEADS * w_uv.shape[2]), jnp.bfloat16),
        in_specs=[SMEM, VMEM, VMEM],
        out_specs=VMEM,
        scratch_shapes=[
            pltpu.VMEM((CTX, 8, 128), jnp.float32),
            pltpu.VMEM((ROWS, HEADS, LATENT), jnp.float32),
            pltpu.SMEM((REQS,), jnp.int32),
        ],
        compiler_params=PARAMS,
    )(row_request, recv, w_uv)


def on_device(queries, latent_cache, w_uv, w_out, selected, row_request, lengths):
    ctx = lax.axis_index("ctx").astype(jnp.int32).reshape(1)
    dp = lax.axis_index("dp").astype(jnp.int32).reshape(1)
    cache = latent_cache[0]
    pairs = []
    for device in range(CTX * CTX):
        core, y = device // CTX % 2, device % SPAN
        other = y ^ 1 if core == 0 else (y + 1 if y % 2 == 1 else y - 1) % SPAN
        pairs.append((device, device - y + other))
    other_keys = lax.ppermute(cache, ("dp", "ctx"), pairs).reshape(-1, cache.shape[2])
    keys = cache.reshape(-1, cache.shape[2])
    branch = pl.pallas_call(
        plan_kernel,
        out_shape=jax.ShapeDtypeStruct((1,), jnp.int32),
        in_specs=[SMEM],
        out_specs=SMEM,
        scratch_shapes=[pltpu.SMEM((REQS,), jnp.int32)],
    )(row_request)[0]
    recv, bias = lax.switch(
        branch,
        [functools.partial(to_keys, slots, tokens=keys.shape[0]) for slots in SLOTS],
        queries, selected, row_request, lengths[0], ctx, dp,
    )
    recv, bias, other_keys = lax.optimization_barrier((recv, bias, other_keys))
    hidden = lax.switch(
        branch,
        [functools.partial(to_heads, slots) for slots in SLOTS],
        recv, bias, keys, other_keys, w_uv, row_request, ctx,
    )
    hidden = lax.all_gather(hidden, "dp", axis=0, tiled=True)
    partial_out = jnp.dot(hidden, w_out, preferred_element_type=jnp.float32)
    partial_out = partial_out.astype(jnp.bfloat16).reshape(CTX, -1, w_out.shape[1])
    parts = lax.all_to_all(partial_out, "ctx", 0, 0)
    return jnp.sum(parts.astype(jnp.float32), axis=0).astype(jnp.bfloat16)


def solution(mesh):
    in_specs = (
        P("dp", "ctx", None),
        P("dp", "ctx", None, None),
        P("ctx", None, None),
        P("ctx", "dp"),
        P("dp", None),
        P("dp"),
        P("dp", None),
    )
    out_specs = P("ctx", "dp")
    return jax.shard_map(
        on_device, mesh=mesh, in_specs=in_specs, out_specs=out_specs, check_vma=False
    )
```

```python
import functools

import jax
import jax.numpy as jnp
from jax import lax
from jax.experimental import pallas as pl
from jax.experimental.pallas import tpu as pltpu
from jax.sharding import PartitionSpec as P

REQ_BLOCKS = 64
ROWS = 16
REQS = 4
SLOTS = (7, 10, 14)
HEADS = 8
HALF = 4
CTX = 16
SPAN = CTX // REQS
LATENT = 512
ROPE = 64
FLOOR = -300000.0
SCALE = 192.0**-0.5 * 1.4426950408889634
MASKED = -1e30
LO, HI = 64, 32

VMEM = pl.BlockSpec(memory_space=pltpu.VMEM)
SMEM = pl.BlockSpec(memory_space=pltpu.SMEM)


def message_rows(slots):
    return -(-(slots + 1) // 2) * 8 if slots < 8 else slots * HALF + 8


def partner(y, core):
    return jnp.where(core == 0, y ^ 1, (y + 1 - 2 * (1 - y % 2)) % SPAN)


def upper(shape, axis):
    return lax.broadcasted_iota(jnp.int32, shape, axis) < HALF


def pack_kernel(
    ctx_ref, dp_ref, request_ref, lengths_ref, selected_ref, queries_ref, *refs,
):
    out_refs, (branch_ref, bias_ref, nope, rope, bias, count) = refs[: len(SLOTS)], refs[len(SLOTS) :]
    rope[...] = jnp.zeros_like(rope)
    for x in range(REQS):
        count[x] = 0
    x, y = ctx_ref[0] // SPAN, ctx_ref[0] % SPAN
    places = (y, partner(y, dp_ref[0] % 2))
    tokens = bias_ref.shape[2]
    for i in range(2):
        token = lax.broadcasted_iota(jnp.int32, (ROWS, tokens), 1) + places[i] * tokens
        block = token // (tokens // 16)
        chosen = selected_ref[:, 0:1] == block
        for k in range(1, selected_ref.shape[1]):
            chosen = chosen | (selected_ref[:, k : k + 1] == block)
        bias[i] = jnp.where(chosen & (token < lengths_ref[x]), 0.0, MASKED)
        bias_ref[i] = jnp.full((bias_ref.shape[1], tokens), MASKED, jnp.float32)
    for r in range(ROWS):
        x = request_ref[r]
        s = count[x]
        count[x] = s + 1
        q = queries_ref[r].astype(jnp.float32)
        moved = pltpu.roll(q, HALF, 0)
        tile = pl.ds(pl.multiple_of(s // 2 * 8, 8), 8)
        lanes = pl.ds(pl.multiple_of(s % 8 // 2 * 128, 128), 128)
        first = upper((8, LATENT), 0) == (s % 2 == 0)
        spot = lax.broadcasted_iota(jnp.int32, (8, 128), 1) < ROPE
        spot = (spot == (s % 2 == 0)) & (upper((8, 128), 0) == (s < 8))
        for h in range(2):
            value = jnp.where(s % 2 == h, q[:, :LATENT], moved[:, :LATENT])
            nope[x, h, tile, :] = jnp.where(first, value, nope[x, h, tile, :])
            part = jnp.where(s // 8 == h, q[:, LATENT:], moved[:, LATENT:])
            part = jnp.concatenate([part, part], axis=1)
            rope[x, h, :, lanes] = rope[x, h, :, lanes] + jnp.where(spot, part, 0.0)
        own = jnp.where(x == ctx_ref[0] // SPAN, s, ROWS)
        for i in range(2):
            bias_ref[i, pl.ds(own, 1), :] = bias[i, r : r + 1, :]
    needed = functools.reduce(jnp.maximum, [count[x] for x in range(REQS)])
    branch = sum((needed > slots).astype(jnp.int32) for slots in SLOTS[:-1])
    branch_ref[0] = branch
    quads = ((needed + 3) // 4).astype(jnp.float32)
    bias_ref[0, ROWS : ROWS + 8, :] = jnp.full((8, tokens), quads)

    def write(slots, out_ref):
        size = -(-slots // 2) * 8
        for x in range(REQS):
            for h in range(2):
                if slots % 2 == 1:
                    last = jnp.where(
                        upper((8, LATENT), 0),
                        nope[x, h, size - 8 : size, :],
                        pltpu.roll(rope[x, h], HALF, 0),
                    )
                    full = jnp.concatenate([nope[x, h, : size - 8, :], last], axis=0)
                else:
                    full = jnp.concatenate([nope[x, h, :size, :], rope[x, h]], axis=0)
                full = full.astype(jnp.bfloat16)
                for y in range(h, SPAN, 2):
                    out_ref[x * SPAN + y] = full

    for k, slots in enumerate(SLOTS):
        pl.when(branch == k)(functools.partial(write, slots, out_refs[k]))


def attend_kernel(
    slots, recv_ref, bias, own_ref, other_ref, out_ref, rope_keys, extra
):
    tokens = own_ref.shape[0]
    keys = (own_ref, other_ref)
    lane = lax.broadcasted_iota(jnp.int32, (CTX, 8, 128), 2)
    extra[...] = jnp.where(lane < HI, FLOOR, 0.0)
    top = upper((CTX, 8, 128), 1)
    spot = (lane < ROPE) == top
    contract = (((1,), (1,)), ((), ()))
    rope_start = slots * HALF // 8 * 8
    for i in range(2):
        tail = keys[i][:, LATENT:]
        rope_keys[i] = jnp.concatenate([tail, tail], axis=1)

    def quad_step(p, carry):
        rows = pl.ds(pl.multiple_of(p * 16, 16), 16)
        q = recv_ref[:, rows, :].reshape(CTX * 16, LATENT)
        parts = []
        for u in range(2):
            lanes = pl.ds(pl.multiple_of(p % 2 * 256 + u * 128, 128), 128)
            part = recv_ref[:, rope_start // 16 * 16 : rope_start + 8, lanes].astype(jnp.float32)
            part = part[:, -8:]
            moved = pltpu.roll(part, HALF, 1)
            low = (slots % 2 == 1) | (p >= 2)
            part = jnp.where(low == top, moved, part)
            parts.append(jnp.where(spot, part, 0.0))
        qr = jnp.stack(parts, axis=1).reshape(CTX * 16, 128).astype(jnp.bfloat16)
        wide = upper((8, tokens), 0)
        scores = []
        for i in range(2):
            score = lax.dot_general(
                q, keys[i][:, :LATENT], contract, preferred_element_type=jnp.float32
            ) + lax.dot_general(qr, rope_keys[i], contract, preferred_element_type=jnp.float32)
            add = [bias[i, pl.ds(4 * p + j, 1), :] for j in range(4)]
            add = [jnp.where(wide, add[2 * u], add[2 * u + 1]) for u in range(2)]
            scores.append(score.reshape(CTX, 2, 8, tokens) + jnp.stack(add, axis=0)[None])
        peak = [jnp.max(score, axis=3, keepdims=True) for score in scores]
        peak = jnp.maximum(jnp.maximum(peak[0], peak[1]), FLOOR)
        peak = peak.astype(jnp.bfloat16).astype(jnp.float32)
        probs = [jnp.exp2((score - peak) * SCALE) for score in scores]
        total = sum(jnp.sum(prob, axis=3, keepdims=True) for prob in probs)
        numerator = sum(
            jnp.dot(
                probs[i].reshape(CTX * 16, tokens).astype(jnp.bfloat16),
                keys[i][:, :LATENT],
                preferred_element_type=jnp.float32,
            )
            for i in range(2)
        )
        out_ref[:, rows, :] = numerator.astype(jnp.bfloat16).reshape(CTX, 16, LATENT)
        high = total.astype(jnp.bfloat16).astype(jnp.float32)
        low = total - high
        held = extra[...]
        for u in range(2):
            s = 2 * p + u
            held = jnp.where(lane == s, peak[:, u], held)
            held = jnp.where(lane == s + HI, high[:, u], held)
            held = jnp.where(lane == s + LO, low[:, u], held)
        extra[...] = held
        return carry

    quads = 2
    if slots > 8:
        quads = jnp.max(bias[0, ROWS : ROWS + 8, :128]).astype(jnp.int32)
    lax.fori_loop(0, quads, quad_step, 0)
    start = rope_start // 16 * 16
    last = extra[...]
    last = jnp.concatenate([last, pltpu.roll(last, HALF, 1)], axis=2)
    if slots % 2 == 1:
        last = pltpu.roll(last, HALF, 1)
        kept = out_ref[:, start:, :256].astype(jnp.float32)
        last = jnp.concatenate(
            [kept[:, :-8], jnp.where(upper((CTX, 8, 256), 1), kept[:, -8:], last)], axis=1
        )
    elif start < rope_start:
        kept = out_ref[:, start:, :256].astype(jnp.float32)
        last = jnp.concatenate([kept[:, :-8], last], axis=1)
    out_ref[:, start:, :256] = last.astype(jnp.bfloat16)


def combine_kernel(slots, request_ref, recv_ref, w_uv_ref, out_ref, share, latent, count):
    start = slots * HALF // 16 * 16
    top = upper((8, 128), 0)
    for x in range(REQS):
        count[x] = 0
        for h in range(2):
            parts = []
            for y in range(h, SPAN, 2):
                part = recv_ref[x * SPAN + y, start:, :256].astype(jnp.float32)[-8:]
                if slots % 2 == 1:
                    part = pltpu.roll(part, HALF, 0)
                parts.append(
                    jnp.where(top, part[:, :128], pltpu.roll(part[:, 128:], HALF, 0))
                )
            peak = jnp.maximum(parts[0], parts[1])
            scale = [jnp.exp2((part - peak) * SCALE) for part in parts]
            total = sum(
                f * (pltpu.roll(part, 128 - HI, 1) + pltpu.roll(part, 128 - LO, 1))
                for f, part in zip(scale, parts)
            )
            for i in range(2):
                share[x * SPAN + h + 2 * i] = scale[i] / total
    lane = lax.broadcasted_iota(jnp.int32, (8, 128), 1)
    wide = upper((8, LATENT), 0)
    for r in range(ROWS):
        x = request_ref[r]
        s = count[x]
        count[x] = s + 1
        rows = pl.ds(pl.multiple_of(s // 4 * 16, 16), 16)
        values = []
        for h in range(2):
            value = 0.0
            for y in range(h, SPAN, 2):
                both = recv_ref[x * SPAN + y, rows, :].astype(jnp.float32)
                part = jnp.where(s % 4 >= 2, both[8:], both[:8])
                factor = jnp.sum(
                    jnp.where(lane == s // 2, share[x * SPAN + y], 0.0), axis=1, keepdims=True
                )
                value = value + factor * part
            values.append(jnp.where(s % 2 == h, value, pltpu.roll(value, HALF, 0)))
        latent[r] = jnp.where(wide, values[0], values[1])
    width = w_uv_ref.shape[2]
    for h in range(HEADS):
        hidden = jnp.dot(
            latent[:, h, :].astype(jnp.bfloat16), w_uv_ref[h], preferred_element_type=jnp.float32
        )
        out_ref[:, h * width : (h + 1) * width] = hidden.astype(jnp.bfloat16)


PARAMS = pltpu.CompilerParams(vmem_limit_bytes=40 * 1024 * 1024)


def to_keys(index, *messages):
    recv = lax.all_to_all(messages[index], "ctx", 0, 0)
    spare = message_rows(SLOTS[-1]) - recv.shape[1]
    return jnp.pad(recv, ((0, 0), (0, spare), (0, 0)))


def to_heads(slots, recv, bias, keys, other_keys, w_uv, row_request):
    back = pl.pallas_call(
        functools.partial(attend_kernel, slots),
        out_shape=jax.ShapeDtypeStruct((CTX, message_rows(slots), LATENT), jnp.bfloat16),
        in_specs=[VMEM, VMEM, VMEM, VMEM],
        out_specs=VMEM,
        scratch_shapes=[
            pltpu.VMEM((2, keys.shape[0], 2 * ROPE), jnp.bfloat16),
            pltpu.VMEM((CTX, 8, 128), jnp.float32),
        ],
        compiler_params=PARAMS,
    )(recv, bias, keys, other_keys)
    recv = lax.all_to_all(back, "ctx", 0, 0)
    return pl.pallas_call(
        functools.partial(combine_kernel, slots),
        out_shape=jax.ShapeDtypeStruct((ROWS, HEADS * w_uv.shape[2]), jnp.bfloat16),
        in_specs=[SMEM, VMEM, VMEM],
        out_specs=VMEM,
        scratch_shapes=[
            pltpu.VMEM((CTX, 8, 128), jnp.float32),
            pltpu.VMEM((ROWS, HEADS, LATENT), jnp.float32),
            pltpu.SMEM((REQS,), jnp.int32),
        ],
        compiler_params=PARAMS,
    )(row_request, recv, w_uv)


def on_device(queries, latent_cache, w_uv, w_out, selected, row_request, lengths):
    ctx = lax.axis_index("ctx").astype(jnp.int32).reshape(1)
    dp = lax.axis_index("dp").astype(jnp.int32).reshape(1)
    cache = latent_cache[0]
    pairs = []
    for device in range(CTX * CTX):
        core, y = device // CTX % 2, device % SPAN
        other = y ^ 1 if core == 0 else (y + 1 if y % 2 == 1 else y - 1) % SPAN
        pairs.append((device, device - y + other))
    other_keys = lax.ppermute(cache, ("dp", "ctx"), pairs).reshape(-1, cache.shape[2])
    keys = cache.reshape(-1, cache.shape[2])
    *messages, branch, bias = pl.pallas_call(
        pack_kernel,
        out_shape=(
            *(
                jax.ShapeDtypeStruct((CTX, message_rows(slots), LATENT), jnp.bfloat16)
                for slots in SLOTS
            ),
            jax.ShapeDtypeStruct((1,), jnp.int32),
            jax.ShapeDtypeStruct((2, ROWS + 8, keys.shape[0]), jnp.float32),
        ),
        in_specs=[SMEM, SMEM, SMEM, SMEM, VMEM, VMEM],
        out_specs=(*(VMEM for _ in SLOTS), SMEM, VMEM),
        scratch_shapes=[
            pltpu.VMEM((REQS, 2, -(-SLOTS[-1] // 2) * 8, LATENT), jnp.float32),
            pltpu.VMEM((REQS, 2, 8, LATENT), jnp.float32),
            pltpu.VMEM((2, ROWS, keys.shape[0]), jnp.float32),
            pltpu.SMEM((REQS,), jnp.int32),
        ],
        compiler_params=PARAMS,
    )(ctx, dp, row_request, lengths[0], selected, queries)
    branch = branch[0]
    recv = lax.switch(
        branch, [functools.partial(to_keys, index) for index in range(len(SLOTS))], *messages
    )
    recv, other_keys = lax.optimization_barrier((recv, other_keys))
    hidden = lax.switch(
        branch,
        [functools.partial(to_heads, slots) for slots in SLOTS],
        recv, bias, keys, other_keys, w_uv, row_request,
    )
    hidden = lax.all_gather(hidden, "dp", axis=0, tiled=True)
    partial_out = jnp.dot(hidden, w_out, preferred_element_type=jnp.float32)
    partial_out = partial_out.astype(jnp.bfloat16).reshape(CTX, -1, w_out.shape[1])
    parts = lax.all_to_all(partial_out, "ctx", 0, 0)
    return jnp.sum(parts.astype(jnp.float32), axis=0).astype(jnp.bfloat16)


def solution(mesh):
    in_specs = (
        P("dp", "ctx", None),
        P("dp", "ctx", None, None),
        P("ctx", None, None),
        P("ctx", "dp"),
        P("dp", None),
        P("dp"),
        P("dp", None),
    )
    out_specs = P("ctx", "dp")
    return jax.shard_map(
        on_device, mesh=mesh, in_specs=in_specs, out_specs=out_specs, check_vma=False
    )
```

```python
import functools

import jax
import jax.numpy as jnp
from jax import lax
from jax.experimental import pallas as pl
from jax.experimental.pallas import tpu as pltpu
from jax.sharding import PartitionSpec as P

REQ_BLOCKS = 64
ROWS = 16
REQS = 4
SLOTS = (7, 10, 14)
HEADS = 8
CTX = 16
SPAN = CTX // REQS
PEERS = CTX // 2
LATENT = 512
ROPE = 64
FLOOR = -300000.0
SCALE = 192.0**-0.5 * 1.4426950408889634
MASKED = -1e30
LO, HI = 64, 32

VMEM = pl.BlockSpec(memory_space=pltpu.VMEM)
SMEM = pl.BlockSpec(memory_space=pltpu.SMEM)


def message_rows(slots):
    return (slots + -(-slots // 8)) * HEADS


def partner(y, core):
    return jnp.where(core == 0, y ^ 1, (y + 1 - 2 * (1 - y % 2)) % SPAN)


def pack_kernel(
    ctx_ref, dp_ref, request_ref, lengths_ref, selected_ref, queries_ref, *refs,
):
    out_refs, (branch_ref, bias_ref, nope, rope, bias, count) = refs[: len(SLOTS)], refs[len(SLOTS) :]
    rope[...] = jnp.zeros_like(rope)
    for x in range(REQS):
        count[x] = 0
    x, y = ctx_ref[0] // SPAN, ctx_ref[0] % SPAN
    places = (y, partner(y, dp_ref[0] % 2))
    tokens = bias_ref.shape[2]
    for i in range(2):
        token = lax.broadcasted_iota(jnp.int32, (ROWS, tokens), 1) + places[i] * tokens
        block = token // (tokens // 16)
        chosen = selected_ref[:, 0:1] == block
        for k in range(1, selected_ref.shape[1]):
            chosen = chosen | (selected_ref[:, k : k + 1] == block)
        bias[i] = jnp.where(chosen & (token < lengths_ref[x]), 0.0, MASKED)
        bias_ref[i] = jnp.full((bias_ref.shape[1], tokens), MASKED, jnp.float32)
    for r in range(ROWS):
        x = request_ref[r]
        s = count[x]
        count[x] = s + 1
        q = queries_ref[r].astype(jnp.float32)
        nope[x, pl.ds(pl.multiple_of(s * HEADS, HEADS), HEADS), :] = q[:, :LATENT]
        part = jnp.concatenate([q[:, LATENT:], q[:, LATENT:]], axis=1)
        spot = lax.broadcasted_iota(jnp.int32, (HEADS, 128), 1) < ROPE
        tile = pl.ds(pl.multiple_of(s // 8 * HEADS, HEADS), HEADS)
        lanes = pl.ds(pl.multiple_of(s % 8 // 2 * 128, 128), 128)
        part = jnp.where(spot == (s % 2 == 0), part, 0.0)
        rope[x, tile, lanes] = rope[x, tile, lanes] + part
        own = jnp.where(x == ctx_ref[0] // SPAN, s, ROWS)
        for i in range(2):
            bias_ref[i, pl.ds(own, 1), :] = bias[i, r : r + 1, :]
    needed = functools.reduce(jnp.maximum, [count[x] for x in range(REQS)])
    branch = sum((needed > slots).astype(jnp.int32) for slots in SLOTS[:-1])
    branch_ref[0] = branch
    quads = ((needed + 3) // 4).astype(jnp.float32)
    bias_ref[0, ROWS : ROWS + 8, :] = jnp.full((8, tokens), quads)

    def write(slots, out_ref):
        size = slots * HEADS
        for x in range(REQS):
            full = jnp.concatenate(
                [nope[x, :size, :], rope[x, : message_rows(slots) - size, :]], axis=0
            ).astype(jnp.bfloat16)
            for t in range(2):
                out_ref[2 * x + t] = full

    for k, slots in enumerate(SLOTS):
        pl.when(branch == k)(functools.partial(write, slots, out_refs[k]))


def attend_kernel(
    slots, recv_ref, bias, own_ref, other_ref, out_ref, rope_keys, extra
):
    tokens = own_ref.shape[0]
    keys = (own_ref, other_ref)
    lane = lax.broadcasted_iota(jnp.int32, (PEERS, HEADS, 128), 2)
    extra[...] = jnp.where(lane < HI, FLOOR, 0.0)
    left = lane < ROPE
    contract = (((1,), (1,)), ((), ()))
    start = slots * HEADS // 16 * 16
    for i in range(2):
        tail = keys[i][:, LATENT:]
        rope_keys[i] = jnp.concatenate([tail, tail], axis=1)

    def quad_step(p, carry):
        rows = pl.ds(pl.multiple_of(p * 32, 32), 32)
        q = recv_ref[:, rows, :].reshape(PEERS * 32, LATENT)
        parts = []
        for u in range(2):
            lanes = pl.ds(pl.multiple_of(p % 2 * 256 + u * 128, 128), 128)
            part = recv_ref[:, start : start + 16, lanes].astype(jnp.float32)
            if slots % 2 == 1:
                part = part[:, 8:]
            else:
                part = jnp.where(p < 2, part[:, :8], part[:, 8:])
            parts.append(jnp.where(left, part, 0.0))
            parts.append(jnp.where(left, 0.0, part))
        qr = jnp.stack(parts, axis=1).reshape(PEERS * 32, 128).astype(jnp.bfloat16)
        scores = []
        for i in range(2):
            score = lax.dot_general(
                q, keys[i][:, :LATENT], contract, preferred_element_type=jnp.float32
            ) + lax.dot_general(qr, rope_keys[i], contract, preferred_element_type=jnp.float32)
            add = jnp.stack([bias[i, pl.ds(4 * p + j, 1), :] for j in range(4)], axis=0)
            scores.append(score.reshape(PEERS, 4, HEADS, tokens) + add[None])
        peak = [jnp.max(score, axis=3, keepdims=True) for score in scores]
        peak = jnp.maximum(jnp.maximum(peak[0], peak[1]), FLOOR)
        peak = peak.astype(jnp.bfloat16).astype(jnp.float32)
        probs = [jnp.exp2((score - peak) * SCALE) for score in scores]
        total = sum(jnp.sum(prob, axis=3, keepdims=True) for prob in probs)
        numerator = sum(
            jnp.dot(
                probs[i].reshape(PEERS * 32, tokens).astype(jnp.bfloat16),
                keys[i][:, :LATENT],
                preferred_element_type=jnp.float32,
            )
            for i in range(2)
        )
        out_ref[:, rows, :] = numerator.astype(jnp.bfloat16).reshape(PEERS, 32, LATENT)
        high = total.astype(jnp.bfloat16).astype(jnp.float32)
        low = total - high
        held = extra[...]
        for j in range(4):
            s = 4 * p + j
            held = jnp.where(lane == s, peak[:, j], held)
            held = jnp.where(lane == s + HI, high[:, j], held)
            held = jnp.where(lane == s + LO, low[:, j], held)
        extra[...] = held
        return carry

    quads = 2
    if slots > 8:
        quads = jnp.max(bias[0, ROWS : ROWS + 8, :128]).astype(jnp.int32)
    lax.fori_loop(0, quads, quad_step, 0)
    last = extra[...]
    kept = out_ref[:, start : start + 16, :128].astype(jnp.float32)
    if slots % 2 == 1:
        last = jnp.concatenate([kept[:, :8], last], axis=1)
    else:
        last = jnp.concatenate([last, kept[:, 8:]], axis=1)
    out_ref[:, start : start + 16, :128] = last.astype(jnp.bfloat16)


def combine_kernel(slots, request_ref, recv_ref, w_uv_ref, out_ref, share, latent, count):
    start = slots * HEADS // 16 * 16
    first = slots * HEADS - start
    for x in range(REQS):
        count[x] = 0
        parts = [
            recv_ref[2 * x + t, start : start + 16, :128].astype(jnp.float32)[first : first + 8]
            for t in range(2)
        ]
        peak = jnp.maximum(parts[0], parts[1])
        scale = [jnp.exp2((part - peak) * SCALE) for part in parts]
        total = sum(
            f * (pltpu.roll(part, 128 - HI, 1) + pltpu.roll(part, 128 - LO, 1))
            for f, part in zip(scale, parts)
        )
        for t in range(2):
            share[2 * x + t] = scale[t] / total
    lane = lax.broadcasted_iota(jnp.int32, (HEADS, 128), 1)
    for r in range(ROWS):
        x = request_ref[r]
        s = count[x]
        count[x] = s + 1
        rows = pl.ds(pl.multiple_of(s // 2 * 16, 16), 16)
        value = 0.0
        for t in range(2):
            both = recv_ref[2 * x + t, rows, :].astype(jnp.float32)
            part = jnp.where(s % 2 == 1, both[8:], both[:8])
            factor = jnp.sum(
                jnp.where(lane == s, share[2 * x + t], 0.0), axis=1, keepdims=True
            )
            value = value + factor * part
        latent[r] = value
    width = w_uv_ref.shape[2]
    for h in range(HEADS):
        hidden = jnp.dot(
            latent[:, h, :].astype(jnp.bfloat16), w_uv_ref[h], preferred_element_type=jnp.float32
        )
        out_ref[:, h * width : (h + 1) * width] = hidden.astype(jnp.bfloat16)


PARAMS = pltpu.CompilerParams(vmem_limit_bytes=40 * 1024 * 1024)


def exchange(message):
    groups = []
    for group in range(CTX):
        for ys in ((0, 3), (1, 2)) if group % 2 == 0 else ((0, 1), (2, 3)):
            groups.append([group * CTX + x * SPAN + y for x in range(REQS) for y in ys])
    return lax.all_to_all(message, ("dp", "ctx"), 0, 0, axis_index_groups=groups)


def to_keys(index, *messages):
    recv = exchange(messages[index])
    spare = message_rows(SLOTS[-1]) - recv.shape[1]
    return jnp.pad(recv, ((0, 0), (0, spare), (0, 0)))


def to_heads(slots, recv, bias, keys, other_keys, w_uv, row_request):
    back = pl.pallas_call(
        functools.partial(attend_kernel, slots),
        out_shape=jax.ShapeDtypeStruct((PEERS, message_rows(slots), LATENT), jnp.bfloat16),
        in_specs=[VMEM, VMEM, VMEM, VMEM],
        out_specs=VMEM,
        scratch_shapes=[
            pltpu.VMEM((2, keys.shape[0], 2 * ROPE), jnp.bfloat16),
            pltpu.VMEM((PEERS, HEADS, 128), jnp.float32),
        ],
        compiler_params=PARAMS,
    )(recv, bias, keys, other_keys)
    recv = exchange(back)
    return pl.pallas_call(
        functools.partial(combine_kernel, slots),
        out_shape=jax.ShapeDtypeStruct((ROWS, HEADS * w_uv.shape[2]), jnp.bfloat16),
        in_specs=[SMEM, VMEM, VMEM],
        out_specs=VMEM,
        scratch_shapes=[
            pltpu.VMEM((PEERS, HEADS, 128), jnp.float32),
            pltpu.VMEM((ROWS, HEADS, LATENT), jnp.float32),
            pltpu.SMEM((REQS,), jnp.int32),
        ],
        compiler_params=PARAMS,
    )(row_request, recv, w_uv)


def on_device(queries, latent_cache, w_uv, w_out, selected, row_request, lengths):
    ctx = lax.axis_index("ctx").astype(jnp.int32).reshape(1)
    dp = lax.axis_index("dp").astype(jnp.int32).reshape(1)
    cache = latent_cache[0]
    pairs = []
    for device in range(CTX * CTX):
        core, y = device // CTX % 2, device % SPAN
        other = y ^ 1 if core == 0 else (y + 1 if y % 2 == 1 else y - 1) % SPAN
        pairs.append((device, device - y + other))
    other_keys = lax.ppermute(cache, ("dp", "ctx"), pairs).reshape(-1, cache.shape[2])
    keys = cache.reshape(-1, cache.shape[2])
    *messages, branch, bias = pl.pallas_call(
        pack_kernel,
        out_shape=(
            *(
                jax.ShapeDtypeStruct((PEERS, message_rows(slots), LATENT), jnp.bfloat16)
                for slots in SLOTS
            ),
            jax.ShapeDtypeStruct((1,), jnp.int32),
            jax.ShapeDtypeStruct((2, ROWS + 8, keys.shape[0]), jnp.float32),
        ),
        in_specs=[SMEM, SMEM, SMEM, SMEM, VMEM, VMEM],
        out_specs=(*(VMEM for _ in SLOTS), SMEM, VMEM),
        scratch_shapes=[
            pltpu.VMEM((REQS, SLOTS[-1] * HEADS, LATENT), jnp.float32),
            pltpu.VMEM((REQS, 2 * HEADS, LATENT), jnp.float32),
            pltpu.VMEM((2, ROWS, keys.shape[0]), jnp.float32),
            pltpu.SMEM((REQS,), jnp.int32),
        ],
        compiler_params=PARAMS,
    )(ctx, dp, row_request, lengths[0], selected, queries)
    branch = branch[0]
    recv = lax.switch(
        branch, [functools.partial(to_keys, index) for index in range(len(SLOTS))], *messages
    )
    recv, other_keys = lax.optimization_barrier((recv, other_keys))
    hidden = lax.switch(
        branch,
        [functools.partial(to_heads, slots) for slots in SLOTS],
        recv, bias, keys, other_keys, w_uv, row_request,
    )
    hidden = lax.all_gather(hidden, "dp", axis=0, tiled=True)
    partial_out = jnp.dot(hidden, w_out, preferred_element_type=jnp.float32)
    partial_out = partial_out.astype(jnp.bfloat16).reshape(CTX, -1, w_out.shape[1])
    parts = lax.all_to_all(partial_out, "ctx", 0, 0)
    return jnp.sum(parts.astype(jnp.float32), axis=0).astype(jnp.bfloat16)


def solution(mesh):
    in_specs = (
        P("dp", "ctx", None),
        P("dp", "ctx", None, None),
        P("ctx", None, None),
        P("ctx", "dp"),
        P("dp", None),
        P("dp"),
        P("dp", None),
    )
    out_specs = P("ctx", "dp")
    return jax.shard_map(
        on_device, mesh=mesh, in_specs=in_specs, out_specs=out_specs, check_vma=False
    )
```

```python
import functools

import jax
import jax.numpy as jnp
from jax import lax
from jax.experimental import pallas as pl
from jax.experimental.pallas import tpu as pltpu
from jax.sharding import PartitionSpec as P

REQ_BLOCKS = 64
ROWS = 16
REQS = 4
SLOTS = (7, 10, 14)
HEADS = 8
CTX = 16
SPAN = CTX // REQS
PEERS = CTX // 2
LATENT = 512
ROPE = 64
FLOOR = -300000.0
SCALE = 192.0**-0.5 * 1.4426950408889634
MASKED = -1e30
LO, HI = 64, 32

VMEM = pl.BlockSpec(memory_space=pltpu.VMEM)
SMEM = pl.BlockSpec(memory_space=pltpu.SMEM)


def message_rows(slots):
    return (slots + -(-slots // 8)) * HEADS


def partner(y, core):
    return jnp.where(core == 0, y ^ 1, (y + 1 - 2 * (1 - y % 2)) % SPAN)


def pack_kernel(
    ctx_ref, dp_ref, request_ref, lengths_ref, selected_ref, queries_ref, *refs,
):
    out_refs, (branch_ref, bias_ref, nope, rope, bias, count) = refs[: len(SLOTS)], refs[len(SLOTS) :]
    rope[...] = jnp.zeros_like(rope)
    for x in range(REQS):
        count[x] = 0
    x, y = ctx_ref[0] // SPAN, ctx_ref[0] % SPAN
    places = (y, partner(y, dp_ref[0] % 2))
    tokens = bias_ref.shape[2]
    for i in range(2):
        token = lax.broadcasted_iota(jnp.int32, (ROWS, tokens), 1) + places[i] * tokens
        block = token // (tokens // 16)
        chosen = selected_ref[:, 0:1] == block
        for k in range(1, selected_ref.shape[1]):
            chosen = chosen | (selected_ref[:, k : k + 1] == block)
        bias[i] = jnp.where(chosen & (token < lengths_ref[x]), 0.0, MASKED)
        bias_ref[i] = jnp.full((bias_ref.shape[1], tokens), MASKED, jnp.float32)
    for r in range(ROWS):
        x = request_ref[r]
        s = count[x]
        count[x] = s + 1
        q = queries_ref[r].astype(jnp.float32)
        nope[x, pl.ds(pl.multiple_of(s * HEADS, HEADS), HEADS), :] = q[:, :LATENT]
        part = jnp.concatenate([q[:, LATENT:], q[:, LATENT:]], axis=1)
        spot = lax.broadcasted_iota(jnp.int32, (HEADS, 128), 1) < ROPE
        tile = pl.ds(pl.multiple_of(s // 8 * HEADS, HEADS), HEADS)
        lanes = pl.ds(pl.multiple_of(s % 8 // 2 * 128, 128), 128)
        part = jnp.where(spot == (s % 2 == 0), part, 0.0)
        rope[x, tile, lanes] = rope[x, tile, lanes] + part
        own = jnp.where(x == ctx_ref[0] // SPAN, s, ROWS)
        for i in range(2):
            bias_ref[i, pl.ds(own, 1), :] = bias[i, r : r + 1, :]
    needed = functools.reduce(jnp.maximum, [count[x] for x in range(REQS)])
    branch = sum((needed > slots).astype(jnp.int32) for slots in SLOTS[:-1])
    branch_ref[0] = branch
    quads = ((needed + 3) // 4).astype(jnp.float32)
    bias_ref[0, ROWS : ROWS + 8, :] = jnp.full((8, tokens), quads)

    def write(slots, out_ref):
        size = slots * HEADS
        for x in range(REQS):
            full = jnp.concatenate(
                [nope[x, :size, :], rope[x, : message_rows(slots) - size, :]], axis=0
            ).astype(jnp.bfloat16)
            for t in range(2):
                out_ref[2 * x + t] = full

    for k, slots in enumerate(SLOTS):
        pl.when(branch == k)(functools.partial(write, slots, out_refs[k]))


def attend_kernel(
    slots, recv_ref, bias, own_ref, other_ref, out_ref, other, rope_keys, extra, arrived
):
    tokens = own_ref.shape[0]
    copy = pltpu.make_async_copy(other_ref, other, arrived)
    copy.start()
    keys = (own_ref, other)
    lane = lax.broadcasted_iota(jnp.int32, (PEERS, HEADS, 128), 2)
    extra[...] = jnp.where(lane < HI, FLOOR, 0.0)
    left = lane < ROPE
    contract = (((1,), (1,)), ((), ()))
    start = slots * HEADS // 16 * 16
    def double_rope(i):
        tail = keys[i][:, LATENT:]
        rope_keys[i] = jnp.concatenate([tail, tail], axis=1)

    double_rope(0)

    def quad_step(p, carry, first=False):
        rows = pl.ds(pl.multiple_of(p * 32, 32), 32)
        q = recv_ref[:, rows, :].reshape(PEERS * 32, LATENT)
        parts = []
        for u in range(2):
            lanes = pl.ds(pl.multiple_of(p % 2 * 256 + u * 128, 128), 128)
            part = recv_ref[:, start : start + 16, lanes].astype(jnp.float32)
            if slots % 2 == 1:
                part = part[:, 8:]
            else:
                part = jnp.where(p < 2, part[:, :8], part[:, 8:])
            parts.append(jnp.where(left, part, 0.0))
            parts.append(jnp.where(left, 0.0, part))
        qr = jnp.stack(parts, axis=1).reshape(PEERS * 32, 128).astype(jnp.bfloat16)
        scores = []
        for i in range(2):
            if i == 1 and first:
                copy.wait()
                double_rope(1)
            score = lax.dot_general(
                q, keys[i][:, :LATENT], contract, preferred_element_type=jnp.float32
            ) + lax.dot_general(qr, rope_keys[i], contract, preferred_element_type=jnp.float32)
            add = jnp.stack([bias[i, pl.ds(4 * p + j, 1), :] for j in range(4)], axis=0)
            scores.append(score.reshape(PEERS, 4, HEADS, tokens) + add[None])
        peak = [jnp.max(score, axis=3, keepdims=True) for score in scores]
        peak = jnp.maximum(jnp.maximum(peak[0], peak[1]), FLOOR)
        peak = peak.astype(jnp.bfloat16).astype(jnp.float32)
        probs = [jnp.exp2((score - peak) * SCALE) for score in scores]
        total = sum(jnp.sum(prob, axis=3, keepdims=True) for prob in probs)
        numerator = sum(
            jnp.dot(
                probs[i].reshape(PEERS * 32, tokens).astype(jnp.bfloat16),
                keys[i][:, :LATENT],
                preferred_element_type=jnp.float32,
            )
            for i in range(2)
        )
        out_ref[:, rows, :] = numerator.astype(jnp.bfloat16).reshape(PEERS, 32, LATENT)
        high = total.astype(jnp.bfloat16).astype(jnp.float32)
        low = total - high
        held = extra[...]
        for j in range(4):
            s = 4 * p + j
            held = jnp.where(lane == s, peak[:, j], held)
            held = jnp.where(lane == s + HI, high[:, j], held)
            held = jnp.where(lane == s + LO, low[:, j], held)
        extra[...] = held
        return carry

    quads = 2
    if slots > 8:
        quads = jnp.max(bias[0, ROWS : ROWS + 8, :128]).astype(jnp.int32)
    quad_step(0, 0, first=True)
    lax.fori_loop(1, quads, quad_step, 0)
    last = extra[...]
    kept = out_ref[:, start : start + 16, :128].astype(jnp.float32)
    if slots % 2 == 1:
        last = jnp.concatenate([kept[:, :8], last], axis=1)
    else:
        last = jnp.concatenate([last, kept[:, 8:]], axis=1)
    out_ref[:, start : start + 16, :128] = last.astype(jnp.bfloat16)


def combine_kernel(slots, request_ref, recv_ref, w_uv_ref, out_ref, share, latent, count):
    start = slots * HEADS // 16 * 16
    first = slots * HEADS - start
    for x in range(REQS):
        count[x] = 0
        parts = [
            recv_ref[2 * x + t, start : start + 16, :128].astype(jnp.float32)[first : first + 8]
            for t in range(2)
        ]
        peak = jnp.maximum(parts[0], parts[1])
        scale = [jnp.exp2((part - peak) * SCALE) for part in parts]
        total = sum(
            f * (pltpu.roll(part, 128 - HI, 1) + pltpu.roll(part, 128 - LO, 1))
            for f, part in zip(scale, parts)
        )
        for t in range(2):
            share[2 * x + t] = scale[t] / total
    lane = lax.broadcasted_iota(jnp.int32, (HEADS, 128), 1)
    for r in range(ROWS):
        x = request_ref[r]
        s = count[x]
        count[x] = s + 1
        rows = pl.ds(pl.multiple_of(s // 2 * 16, 16), 16)
        value = 0.0
        for t in range(2):
            both = recv_ref[2 * x + t, rows, :].astype(jnp.float32)
            part = jnp.where(s % 2 == 1, both[8:], both[:8])
            factor = jnp.sum(
                jnp.where(lane == s, share[2 * x + t], 0.0), axis=1, keepdims=True
            )
            value = value + factor * part
        latent[r] = value
    width = w_uv_ref.shape[2]
    for h in range(HEADS):
        hidden = jnp.dot(
            latent[:, h, :].astype(jnp.bfloat16), w_uv_ref[h], preferred_element_type=jnp.float32
        )
        out_ref[:, h * width : (h + 1) * width] = hidden.astype(jnp.bfloat16)


PARAMS = pltpu.CompilerParams(vmem_limit_bytes=40 * 1024 * 1024)


def exchange(message):
    groups = []
    for group in range(CTX):
        for ys in ((0, 3), (1, 2)) if group % 2 == 0 else ((0, 1), (2, 3)):
            groups.append([group * CTX + x * SPAN + y for x in range(REQS) for y in ys])
    return lax.all_to_all(message, ("dp", "ctx"), 0, 0, axis_index_groups=groups)


def to_keys(index, *messages):
    recv = exchange(messages[index])
    spare = message_rows(SLOTS[-1]) - recv.shape[1]
    return jnp.pad(recv, ((0, 0), (0, spare), (0, 0)))


def to_heads(slots, recv, bias, keys, other_keys, w_uv, row_request):
    back = pl.pallas_call(
        functools.partial(attend_kernel, slots),
        out_shape=jax.ShapeDtypeStruct((PEERS, message_rows(slots), LATENT), jnp.bfloat16),
        in_specs=[VMEM, VMEM, VMEM, pl.BlockSpec(memory_space=pl.ANY)],
        out_specs=VMEM,
        scratch_shapes=[
            pltpu.VMEM(keys.shape, jnp.bfloat16),
            pltpu.VMEM((2, keys.shape[0], 2 * ROPE), jnp.bfloat16),
            pltpu.VMEM((PEERS, HEADS, 128), jnp.float32),
            pltpu.SemaphoreType.DMA,
        ],
        compiler_params=PARAMS,
    )(recv, bias, keys, other_keys)
    recv = exchange(back)
    return pl.pallas_call(
        functools.partial(combine_kernel, slots),
        out_shape=jax.ShapeDtypeStruct((ROWS, HEADS * w_uv.shape[2]), jnp.bfloat16),
        in_specs=[SMEM, VMEM, VMEM],
        out_specs=VMEM,
        scratch_shapes=[
            pltpu.VMEM((PEERS, HEADS, 128), jnp.float32),
            pltpu.VMEM((ROWS, HEADS, LATENT), jnp.float32),
            pltpu.SMEM((REQS,), jnp.int32),
        ],
        compiler_params=PARAMS,
    )(row_request, recv, w_uv)


def on_device(queries, latent_cache, w_uv, w_out, selected, row_request, lengths):
    ctx = lax.axis_index("ctx").astype(jnp.int32).reshape(1)
    dp = lax.axis_index("dp").astype(jnp.int32).reshape(1)
    cache = latent_cache[0]
    pairs = []
    for device in range(CTX * CTX):
        core, y = device // CTX % 2, device % SPAN
        other = y ^ 1 if core == 0 else (y + 1 if y % 2 == 1 else y - 1) % SPAN
        pairs.append((device, device - y + other))
    other_keys = lax.ppermute(cache, ("dp", "ctx"), pairs).reshape(-1, cache.shape[2])
    keys = cache.reshape(-1, cache.shape[2])
    *messages, branch, bias = pl.pallas_call(
        pack_kernel,
        out_shape=(
            *(
                jax.ShapeDtypeStruct((PEERS, message_rows(slots), LATENT), jnp.bfloat16)
                for slots in SLOTS
            ),
            jax.ShapeDtypeStruct((1,), jnp.int32),
            jax.ShapeDtypeStruct((2, ROWS + 8, keys.shape[0]), jnp.float32),
        ),
        in_specs=[SMEM, SMEM, SMEM, SMEM, VMEM, VMEM],
        out_specs=(*(VMEM for _ in SLOTS), SMEM, VMEM),
        scratch_shapes=[
            pltpu.VMEM((REQS, SLOTS[-1] * HEADS, LATENT), jnp.float32),
            pltpu.VMEM((REQS, 2 * HEADS, LATENT), jnp.float32),
            pltpu.VMEM((2, ROWS, keys.shape[0]), jnp.float32),
            pltpu.SMEM((REQS,), jnp.int32),
        ],
        compiler_params=PARAMS,
    )(ctx, dp, row_request, lengths[0], selected, queries)
    branch = branch[0]
    recv = lax.switch(
        branch, [functools.partial(to_keys, index) for index in range(len(SLOTS))], *messages
    )
    recv, other_keys = lax.optimization_barrier((recv, other_keys))
    hidden = lax.switch(
        branch,
        [functools.partial(to_heads, slots) for slots in SLOTS],
        recv, bias, keys, other_keys, w_uv, row_request,
    )
    hidden = lax.all_gather(hidden, "dp", axis=0, tiled=True)
    partial_out = jnp.dot(hidden, w_out, preferred_element_type=jnp.float32)
    partial_out = partial_out.astype(jnp.bfloat16).reshape(CTX, -1, w_out.shape[1])
    parts = lax.all_to_all(partial_out, "ctx", 0, 0)
    return jnp.sum(parts.astype(jnp.float32), axis=0).astype(jnp.bfloat16)


def solution(mesh):
    in_specs = (
        P("dp", "ctx", None),
        P("dp", "ctx", None, None),
        P("ctx", None, None),
        P("ctx", "dp"),
        P("dp", None),
        P("dp"),
        P("dp", None),
    )
    out_specs = P("ctx", "dp")
    return jax.shard_map(
        on_device, mesh=mesh, in_specs=in_specs, out_specs=out_specs, check_vma=False
    )
```

```python
import functools

import jax
import jax.numpy as jnp
from jax import lax
from jax.experimental import pallas as pl
from jax.experimental.pallas import tpu as pltpu
from jax.sharding import PartitionSpec as P

REQ_BLOCKS = 64
ROWS = 16
REQS = 4
SLOTS = (7, 10, 14)
HEADS = 8
CTX = 16
SPAN = CTX // REQS
PEERS = CTX // 2
LATENT = 512
ROPE = 64
FLOOR = -300000.0
SCALE = 192.0**-0.5 * 1.4426950408889634
MASKED = -1e30
LO, HI = 64, 32

VMEM = pl.BlockSpec(memory_space=pltpu.VMEM)
SMEM = pl.BlockSpec(memory_space=pltpu.SMEM)


def message_rows(slots):
    return (slots + -(-slots // 8)) * HEADS


def partner(y, core):
    return jnp.where(core == 0, y ^ 1, (y + 1 - 2 * (1 - y % 2)) % SPAN)


def pack_kernel(
    ctx_ref, dp_ref, request_ref, lengths_ref, selected_ref, queries_hbm, *refs,
):
    out_refs, (branch_ref, bias_ref, *scratch) = refs[: len(SLOTS)], refs[len(SLOTS) :]
    nope, rope, bias, count, queries_ref, arrived = scratch
    copy = pltpu.make_async_copy(queries_hbm, queries_ref, arrived)
    copy.start()
    rope[...] = jnp.zeros_like(rope)
    for x in range(REQS):
        count[x] = 0
    x, y = ctx_ref[0] // SPAN, ctx_ref[0] % SPAN
    places = (y, partner(y, dp_ref[0] % 2))
    tokens = bias_ref.shape[2]
    for i in range(2):
        token = lax.broadcasted_iota(jnp.int32, (ROWS, tokens), 1) + places[i] * tokens
        block = token // (tokens // 16)
        chosen = selected_ref[:, 0:1] == block
        for k in range(1, selected_ref.shape[1]):
            chosen = chosen | (selected_ref[:, k : k + 1] == block)
        bias[i] = jnp.where(chosen & (token < lengths_ref[x]), 0.0, MASKED)
        bias_ref[i] = jnp.full((bias_ref.shape[1], tokens), MASKED, jnp.float32)
    copy.wait()
    for r in range(ROWS):
        x = request_ref[r]
        s = count[x]
        count[x] = s + 1
        q = queries_ref[r].astype(jnp.float32)
        nope[x, pl.ds(pl.multiple_of(s * HEADS, HEADS), HEADS), :] = q[:, :LATENT]
        part = jnp.concatenate([q[:, LATENT:], q[:, LATENT:]], axis=1)
        spot = lax.broadcasted_iota(jnp.int32, (HEADS, 128), 1) < ROPE
        tile = pl.ds(pl.multiple_of(s // 8 * HEADS, HEADS), HEADS)
        lanes = pl.ds(pl.multiple_of(s % 8 // 2 * 128, 128), 128)
        part = jnp.where(spot == (s % 2 == 0), part, 0.0)
        rope[x, tile, lanes] = rope[x, tile, lanes] + part
        own = jnp.where(x == ctx_ref[0] // SPAN, s, ROWS)
        for i in range(2):
            bias_ref[i, pl.ds(own, 1), :] = bias[i, r : r + 1, :]
    needed = functools.reduce(jnp.maximum, [count[x] for x in range(REQS)])
    branch = sum((needed > slots).astype(jnp.int32) for slots in SLOTS[:-1])
    branch_ref[0] = branch
    quads = ((needed + 3) // 4).astype(jnp.float32)
    bias_ref[0, ROWS : ROWS + 8, :] = jnp.full((8, tokens), quads)

    def write(slots, out_ref):
        size = slots * HEADS
        for x in range(REQS):
            full = jnp.concatenate(
                [nope[x, :size, :], rope[x, : message_rows(slots) - size, :]], axis=0
            ).astype(jnp.bfloat16)
            for t in range(2):
                out_ref[2 * x + t] = full

    for k, slots in enumerate(SLOTS):
        pl.when(branch == k)(functools.partial(write, slots, out_refs[k]))


def attend_kernel(
    slots, recv_ref, bias, own_ref, other_ref, out_ref, other, rope_keys, extra, arrived
):
    tokens = own_ref.shape[0]
    copy = pltpu.make_async_copy(other_ref, other, arrived)
    copy.start()
    keys = (own_ref, other)
    lane = lax.broadcasted_iota(jnp.int32, (PEERS, HEADS, 128), 2)
    extra[...] = jnp.where(lane < HI, FLOOR, 0.0)
    left = lane < ROPE
    contract = (((1,), (1,)), ((), ()))
    start = slots * HEADS // 16 * 16
    def double_rope(i):
        tail = keys[i][:, LATENT:]
        rope_keys[i] = jnp.concatenate([tail, tail], axis=1)

    double_rope(0)

    def quad_step(p, carry, first=False):
        rows = pl.ds(pl.multiple_of(p * 32, 32), 32)
        q = recv_ref[:, rows, :].reshape(PEERS * 32, LATENT)
        parts = []
        for u in range(2):
            lanes = pl.ds(pl.multiple_of(p % 2 * 256 + u * 128, 128), 128)
            part = recv_ref[:, start : start + 16, lanes].astype(jnp.float32)
            if slots % 2 == 1:
                part = part[:, 8:]
            else:
                part = jnp.where(p < 2, part[:, :8], part[:, 8:])
            parts.append(jnp.where(left, part, 0.0))
            parts.append(jnp.where(left, 0.0, part))
        qr = jnp.stack(parts, axis=1).reshape(PEERS * 32, 128).astype(jnp.bfloat16)
        scores = []
        for i in range(2):
            if i == 1 and first:
                copy.wait()
                double_rope(1)
            score = lax.dot_general(
                q, keys[i][:, :LATENT], contract, preferred_element_type=jnp.float32
            ) + lax.dot_general(qr, rope_keys[i], contract, preferred_element_type=jnp.float32)
            add = jnp.stack([bias[i, pl.ds(4 * p + j, 1), :] for j in range(4)], axis=0)
            scores.append(score.reshape(PEERS, 4, HEADS, tokens) + add[None])
        peak = [jnp.max(score, axis=3, keepdims=True) for score in scores]
        peak = jnp.maximum(jnp.maximum(peak[0], peak[1]), FLOOR)
        peak = peak.astype(jnp.bfloat16).astype(jnp.float32)
        probs = [jnp.exp2((score - peak) * SCALE) for score in scores]
        total = sum(jnp.sum(prob, axis=3, keepdims=True) for prob in probs)
        numerator = sum(
            jnp.dot(
                probs[i].reshape(PEERS * 32, tokens).astype(jnp.bfloat16),
                keys[i][:, :LATENT],
                preferred_element_type=jnp.float32,
            )
            for i in range(2)
        )
        out_ref[:, rows, :] = numerator.astype(jnp.bfloat16).reshape(PEERS, 32, LATENT)
        high = total.astype(jnp.bfloat16).astype(jnp.float32)
        low = total - high
        held = extra[...]
        for j in range(4):
            s = 4 * p + j
            held = jnp.where(lane == s, peak[:, j], held)
            held = jnp.where(lane == s + HI, high[:, j], held)
            held = jnp.where(lane == s + LO, low[:, j], held)
        extra[...] = held
        return carry

    quads = 2
    if slots > 8:
        quads = jnp.max(bias[0, ROWS : ROWS + 8, :128]).astype(jnp.int32)
    quad_step(0, 0, first=True)
    lax.fori_loop(1, quads, quad_step, 0)
    last = extra[...]
    kept = out_ref[:, start : start + 16, :128].astype(jnp.float32)
    if slots % 2 == 1:
        last = jnp.concatenate([kept[:, :8], last], axis=1)
    else:
        last = jnp.concatenate([last, kept[:, 8:]], axis=1)
    out_ref[:, start : start + 16, :128] = last.astype(jnp.bfloat16)


def combine_kernel(slots, request_ref, recv_ref, w_uv_ref, out_ref, share, latent, count):
    start = slots * HEADS // 16 * 16
    first = slots * HEADS - start
    for x in range(REQS):
        count[x] = 0
        parts = [
            recv_ref[2 * x + t, start : start + 16, :128].astype(jnp.float32)[first : first + 8]
            for t in range(2)
        ]
        peak = jnp.maximum(parts[0], parts[1])
        scale = [jnp.exp2((part - peak) * SCALE) for part in parts]
        total = sum(
            f * (pltpu.roll(part, 128 - HI, 1) + pltpu.roll(part, 128 - LO, 1))
            for f, part in zip(scale, parts)
        )
        for t in range(2):
            share[2 * x + t] = scale[t] / total
    lane = lax.broadcasted_iota(jnp.int32, (HEADS, 128), 1)
    for r in range(ROWS):
        x = request_ref[r]
        s = count[x]
        count[x] = s + 1
        rows = pl.ds(pl.multiple_of(s // 2 * 16, 16), 16)
        value = 0.0
        for t in range(2):
            both = recv_ref[2 * x + t, rows, :].astype(jnp.float32)
            part = jnp.where(s % 2 == 1, both[8:], both[:8])
            factor = jnp.sum(
                jnp.where(lane == s, share[2 * x + t], 0.0), axis=1, keepdims=True
            )
            value = value + factor * part
        latent[r] = value
    width = w_uv_ref.shape[2]
    for h in range(HEADS):
        hidden = jnp.dot(
            latent[:, h, :].astype(jnp.bfloat16), w_uv_ref[h], preferred_element_type=jnp.float32
        )
        out_ref[:, h * width : (h + 1) * width] = hidden.astype(jnp.bfloat16)


PARAMS = pltpu.CompilerParams(vmem_limit_bytes=40 * 1024 * 1024)


def exchange(message):
    groups = []
    for group in range(CTX):
        for ys in ((0, 3), (1, 2)) if group % 2 == 0 else ((0, 1), (2, 3)):
            groups.append([group * CTX + x * SPAN + y for x in range(REQS) for y in ys])
    return lax.all_to_all(message, ("dp", "ctx"), 0, 0, axis_index_groups=groups)


def to_keys(index, *messages):
    recv = exchange(messages[index])
    spare = message_rows(SLOTS[-1]) - recv.shape[1]
    return jnp.pad(recv, ((0, 0), (0, spare), (0, 0)))


def to_heads(slots, recv, bias, keys, other_keys, w_uv, row_request):
    back = pl.pallas_call(
        functools.partial(attend_kernel, slots),
        out_shape=jax.ShapeDtypeStruct((PEERS, message_rows(slots), LATENT), jnp.bfloat16),
        in_specs=[VMEM, VMEM, VMEM, pl.BlockSpec(memory_space=pl.ANY)],
        out_specs=VMEM,
        scratch_shapes=[
            pltpu.VMEM(keys.shape, jnp.bfloat16),
            pltpu.VMEM((2, keys.shape[0], 2 * ROPE), jnp.bfloat16),
            pltpu.VMEM((PEERS, HEADS, 128), jnp.float32),
            pltpu.SemaphoreType.DMA,
        ],
        compiler_params=PARAMS,
    )(recv, bias, keys, other_keys)
    recv = exchange(back)
    return pl.pallas_call(
        functools.partial(combine_kernel, slots),
        out_shape=jax.ShapeDtypeStruct((ROWS, HEADS * w_uv.shape[2]), jnp.bfloat16),
        in_specs=[SMEM, VMEM, VMEM],
        out_specs=VMEM,
        scratch_shapes=[
            pltpu.VMEM((PEERS, HEADS, 128), jnp.float32),
            pltpu.VMEM((ROWS, HEADS, LATENT), jnp.float32),
            pltpu.SMEM((REQS,), jnp.int32),
        ],
        compiler_params=PARAMS,
    )(row_request, recv, w_uv)


def on_device(queries, latent_cache, w_uv, w_out, selected, row_request, lengths):
    ctx = lax.axis_index("ctx").astype(jnp.int32).reshape(1)
    dp = lax.axis_index("dp").astype(jnp.int32).reshape(1)
    cache = latent_cache[0]
    pairs = []
    for device in range(CTX * CTX):
        core, y = device // CTX % 2, device % SPAN
        other = y ^ 1 if core == 0 else (y + 1 if y % 2 == 1 else y - 1) % SPAN
        pairs.append((device, device - y + other))
    other_keys = lax.ppermute(cache, ("dp", "ctx"), pairs).reshape(-1, cache.shape[2])
    keys = cache.reshape(-1, cache.shape[2])
    *messages, branch, bias = pl.pallas_call(
        pack_kernel,
        out_shape=(
            *(
                jax.ShapeDtypeStruct((PEERS, message_rows(slots), LATENT), jnp.bfloat16)
                for slots in SLOTS
            ),
            jax.ShapeDtypeStruct((1,), jnp.int32),
            jax.ShapeDtypeStruct((2, ROWS + 8, keys.shape[0]), jnp.float32),
        ),
        in_specs=[SMEM, SMEM, SMEM, SMEM, VMEM, pl.BlockSpec(memory_space=pl.ANY)],
        out_specs=(*(VMEM for _ in SLOTS), SMEM, VMEM),
        scratch_shapes=[
            pltpu.VMEM((REQS, SLOTS[-1] * HEADS, LATENT), jnp.float32),
            pltpu.VMEM((REQS, 2 * HEADS, LATENT), jnp.float32),
            pltpu.VMEM((2, ROWS, keys.shape[0]), jnp.float32),
            pltpu.SMEM((REQS,), jnp.int32),
            pltpu.VMEM(queries.shape, jnp.bfloat16),
            pltpu.SemaphoreType.DMA,
        ],
        compiler_params=PARAMS,
    )(ctx, dp, row_request, lengths[0], selected, queries)
    branch = branch[0]
    recv = lax.switch(
        branch, [functools.partial(to_keys, index) for index in range(len(SLOTS))], *messages
    )
    recv, other_keys = lax.optimization_barrier((recv, other_keys))
    hidden = lax.switch(
        branch,
        [functools.partial(to_heads, slots) for slots in SLOTS],
        recv, bias, keys, other_keys, w_uv, row_request,
    )
    hidden = lax.all_gather(hidden, "dp", axis=0, tiled=True)
    partial_out = jnp.dot(hidden, w_out, preferred_element_type=jnp.float32)
    partial_out = partial_out.astype(jnp.bfloat16).reshape(CTX, -1, w_out.shape[1])
    parts = lax.all_to_all(partial_out, "ctx", 0, 0)
    return jnp.sum(parts.astype(jnp.float32), axis=0).astype(jnp.bfloat16)


def solution(mesh):
    in_specs = (
        P("dp", "ctx", None),
        P("dp", "ctx", None, None),
        P("ctx", None, None),
        P("ctx", "dp"),
        P("dp", None),
        P("dp"),
        P("dp", None),
    )
    out_specs = P("ctx", "dp")
    return jax.shard_map(
        on_device, mesh=mesh, in_specs=in_specs, out_specs=out_specs, check_vma=False
    )
```

```python
import functools

import jax
import jax.numpy as jnp
from jax import lax
from jax.experimental import pallas as pl
from jax.experimental.pallas import tpu as pltpu
from jax.sharding import PartitionSpec as P

REQ_BLOCKS = 64
ROWS = 16
REQS = 4
SLOTS = (7, 10, 14)
HEADS = 8
CTX = 16
SPAN = CTX // REQS
PEERS = CTX // 2
LATENT = 512
ROPE = 64
FLOOR = -300000.0
SCALE = 192.0**-0.5 * 1.4426950408889634
MASKED = -1e30
LO, HI = 64, 32

VMEM = pl.BlockSpec(memory_space=pltpu.VMEM)
SMEM = pl.BlockSpec(memory_space=pltpu.SMEM)


def message_rows(slots):
    return (slots + -(-slots // 8)) * HEADS


def partner(y, core):
    return jnp.where(core == 0, y ^ 1, (y + 1 - 2 * (1 - y % 2)) % SPAN)


def pack_kernel(
    ctx_ref, dp_ref, request_ref, lengths_ref, selected_ref, queries_ref, *refs,
):
    out_refs, (branch_ref, bias_ref, nope, rope, bias, count) = refs[: len(SLOTS)], refs[len(SLOTS) :]
    rope[...] = jnp.zeros_like(rope)
    for x in range(REQS):
        count[x] = 0
    x, y = ctx_ref[0] // SPAN, ctx_ref[0] % SPAN
    places = (y, partner(y, dp_ref[0] % 2))
    tokens = bias_ref.shape[2]
    for i in range(2):
        token = lax.broadcasted_iota(jnp.int32, (ROWS, tokens), 1) + places[i] * tokens
        block = token // (tokens // 16)
        chosen = selected_ref[:, 0:1] == block
        for k in range(1, selected_ref.shape[1]):
            chosen = chosen | (selected_ref[:, k : k + 1] == block)
        bias[i] = jnp.where(chosen & (token < lengths_ref[x]), 0.0, MASKED)
        bias_ref[i] = jnp.full((bias_ref.shape[1], tokens), MASKED, jnp.float32)
    for r in range(ROWS):
        x = request_ref[r]
        s = count[x]
        count[x] = s + 1
        q = queries_ref[r].astype(jnp.float32)
        nope[x, pl.ds(pl.multiple_of(s * HEADS, HEADS), HEADS), :] = q[:, :LATENT]
        part = jnp.concatenate([q[:, LATENT:], q[:, LATENT:]], axis=1)
        spot = lax.broadcasted_iota(jnp.int32, (HEADS, 128), 1) < ROPE
        tile = pl.ds(pl.multiple_of(s // 8 * HEADS, HEADS), HEADS)
        lanes = pl.ds(pl.multiple_of(s % 8 // 2 * 128, 128), 128)
        part = jnp.where(spot == (s % 2 == 0), part, 0.0)
        rope[x, tile, lanes] = rope[x, tile, lanes] + part
        own = jnp.where(x == ctx_ref[0] // SPAN, s, ROWS)
        for i in range(2):
            bias_ref[i, pl.ds(own, 1), :] = bias[i, r : r + 1, :]
    needed = functools.reduce(jnp.maximum, [count[x] for x in range(REQS)])
    branch = sum((needed > slots).astype(jnp.int32) for slots in SLOTS[:-1])
    branch_ref[0] = branch
    quads = ((needed + 3) // 4).astype(jnp.float32)
    bias_ref[0, ROWS : ROWS + 8, :] = jnp.full((8, tokens), quads)

    def write(slots, out_ref):
        size = slots * HEADS
        for x in range(REQS):
            full = jnp.concatenate(
                [nope[x, :size, :], rope[x, : message_rows(slots) - size, :]], axis=0
            ).astype(jnp.bfloat16)
            for t in range(2):
                out_ref[2 * x + t] = full

    for k, slots in enumerate(SLOTS):
        pl.when(branch == k)(functools.partial(write, slots, out_refs[k]))


def attend_kernel(
    slots, recv_ref, bias, own_ref, other_ref, out_ref, other, rope_keys, extra, arrived
):
    tokens = own_ref.shape[0]
    half = tokens // 2
    copies = [
        pltpu.make_async_copy(other_ref.at[rows], other.at[rows], arrived.at[i])
        for i, rows in enumerate((pl.ds(0, half), pl.ds(half, half)))
    ]
    for copy in copies:
        copy.start()
    keys = (own_ref, other)
    lane = lax.broadcasted_iota(jnp.int32, (PEERS, HEADS, 128), 2)
    extra[...] = jnp.where(lane < HI, FLOOR, 0.0)
    left = lane < ROPE
    contract = (((1,), (1,)), ((), ()))
    start = slots * HEADS // 16 * 16
    def double_rope(i):
        tail = keys[i][:, LATENT:]
        rope_keys[i] = jnp.concatenate([tail, tail], axis=1)

    double_rope(0)

    def quad_step(p, carry, first=False):
        rows = pl.ds(pl.multiple_of(p * 32, 32), 32)
        q = recv_ref[:, rows, :].reshape(PEERS * 32, LATENT)
        parts = []
        for u in range(2):
            lanes = pl.ds(pl.multiple_of(p % 2 * 256 + u * 128, 128), 128)
            part = recv_ref[:, start : start + 16, lanes].astype(jnp.float32)
            if slots % 2 == 1:
                part = part[:, 8:]
            else:
                part = jnp.where(p < 2, part[:, :8], part[:, 8:])
            parts.append(jnp.where(left, part, 0.0))
            parts.append(jnp.where(left, 0.0, part))
        qr = jnp.stack(parts, axis=1).reshape(PEERS * 32, 128).astype(jnp.bfloat16)
        scores = []
        for i in range(2):
            if i == 1 and first:
                for copy in copies:
                    copy.wait()
                double_rope(1)
            score = lax.dot_general(
                q, keys[i][:, :LATENT], contract, preferred_element_type=jnp.float32
            ) + lax.dot_general(qr, rope_keys[i], contract, preferred_element_type=jnp.float32)
            add = jnp.stack([bias[i, pl.ds(4 * p + j, 1), :] for j in range(4)], axis=0)
            scores.append(score.reshape(PEERS, 4, HEADS, tokens) + add[None])
        peak = [jnp.max(score, axis=3, keepdims=True) for score in scores]
        peak = jnp.maximum(jnp.maximum(peak[0], peak[1]), FLOOR)
        peak = peak.astype(jnp.bfloat16).astype(jnp.float32)
        probs = [jnp.exp2((score - peak) * SCALE) for score in scores]
        total = sum(jnp.sum(prob, axis=3, keepdims=True) for prob in probs)
        numerator = sum(
            jnp.dot(
                probs[i].reshape(PEERS * 32, tokens).astype(jnp.bfloat16),
                keys[i][:, :LATENT],
                preferred_element_type=jnp.float32,
            )
            for i in range(2)
        )
        out_ref[:, rows, :] = numerator.astype(jnp.bfloat16).reshape(PEERS, 32, LATENT)
        high = total.astype(jnp.bfloat16).astype(jnp.float32)
        low = total - high
        held = extra[...]
        for j in range(4):
            s = 4 * p + j
            held = jnp.where(lane == s, peak[:, j], held)
            held = jnp.where(lane == s + HI, high[:, j], held)
            held = jnp.where(lane == s + LO, low[:, j], held)
        extra[...] = held
        return carry

    quads = 2
    if slots > 8:
        quads = jnp.max(bias[0, ROWS : ROWS + 8, :128]).astype(jnp.int32)
    quad_step(0, 0, first=True)
    lax.fori_loop(1, quads, quad_step, 0)
    last = extra[...]
    kept = out_ref[:, start : start + 16, :128].astype(jnp.float32)
    if slots % 2 == 1:
        last = jnp.concatenate([kept[:, :8], last], axis=1)
    else:
        last = jnp.concatenate([last, kept[:, 8:]], axis=1)
    out_ref[:, start : start + 16, :128] = last.astype(jnp.bfloat16)


def combine_kernel(slots, request_ref, recv_ref, w_uv_ref, out_ref, share, latent, count):
    start = slots * HEADS // 16 * 16
    first = slots * HEADS - start
    for x in range(REQS):
        count[x] = 0
        parts = [
            recv_ref[2 * x + t, start : start + 16, :128].astype(jnp.float32)[first : first + 8]
            for t in range(2)
        ]
        peak = jnp.maximum(parts[0], parts[1])
        scale = [jnp.exp2((part - peak) * SCALE) for part in parts]
        total = sum(
            f * (pltpu.roll(part, 128 - HI, 1) + pltpu.roll(part, 128 - LO, 1))
            for f, part in zip(scale, parts)
        )
        for t in range(2):
            share[2 * x + t] = scale[t] / total
    lane = lax.broadcasted_iota(jnp.int32, (HEADS, 128), 1)
    for r in range(ROWS):
        x = request_ref[r]
        s = count[x]
        count[x] = s + 1
        rows = pl.ds(pl.multiple_of(s // 2 * 16, 16), 16)
        value = 0.0
        for t in range(2):
            both = recv_ref[2 * x + t, rows, :].astype(jnp.float32)
            part = jnp.where(s % 2 == 1, both[8:], both[:8])
            factor = jnp.sum(
                jnp.where(lane == s, share[2 * x + t], 0.0), axis=1, keepdims=True
            )
            value = value + factor * part
        latent[r] = value
    width = w_uv_ref.shape[2]
    for h in range(HEADS):
        hidden = jnp.dot(
            latent[:, h, :].astype(jnp.bfloat16), w_uv_ref[h], preferred_element_type=jnp.float32
        )
        out_ref[:, h * width : (h + 1) * width] = hidden.astype(jnp.bfloat16)


PARAMS = pltpu.CompilerParams(vmem_limit_bytes=40 * 1024 * 1024)


def exchange(message):
    groups = []
    for group in range(CTX):
        for ys in ((0, 3), (1, 2)) if group % 2 == 0 else ((0, 1), (2, 3)):
            groups.append([group * CTX + x * SPAN + y for x in range(REQS) for y in ys])
    return lax.all_to_all(message, ("dp", "ctx"), 0, 0, axis_index_groups=groups)


def to_keys(index, *messages):
    recv = exchange(messages[index])
    spare = message_rows(SLOTS[-1]) - recv.shape[1]
    return jnp.pad(recv, ((0, 0), (0, spare), (0, 0)))


def to_heads(slots, recv, bias, keys, other_keys, w_uv, row_request):
    back = pl.pallas_call(
        functools.partial(attend_kernel, slots),
        out_shape=jax.ShapeDtypeStruct((PEERS, message_rows(slots), LATENT), jnp.bfloat16),
        in_specs=[VMEM, VMEM, VMEM, pl.BlockSpec(memory_space=pl.ANY)],
        out_specs=VMEM,
        scratch_shapes=[
            pltpu.VMEM(keys.shape, jnp.bfloat16),
            pltpu.VMEM((2, keys.shape[0], 2 * ROPE), jnp.bfloat16),
            pltpu.VMEM((PEERS, HEADS, 128), jnp.float32),
            pltpu.SemaphoreType.DMA((2,)),
        ],
        compiler_params=PARAMS,
    )(recv, bias, keys, other_keys)
    recv = exchange(back)
    return pl.pallas_call(
        functools.partial(combine_kernel, slots),
        out_shape=jax.ShapeDtypeStruct((ROWS, HEADS * w_uv.shape[2]), jnp.bfloat16),
        in_specs=[SMEM, VMEM, VMEM],
        out_specs=VMEM,
        scratch_shapes=[
            pltpu.VMEM((PEERS, HEADS, 128), jnp.float32),
            pltpu.VMEM((ROWS, HEADS, LATENT), jnp.float32),
            pltpu.SMEM((REQS,), jnp.int32),
        ],
        compiler_params=PARAMS,
    )(row_request, recv, w_uv)


def on_device(queries, latent_cache, w_uv, w_out, selected, row_request, lengths):
    ctx = lax.axis_index("ctx").astype(jnp.int32).reshape(1)
    dp = lax.axis_index("dp").astype(jnp.int32).reshape(1)
    cache = latent_cache[0]
    pairs = []
    for device in range(CTX * CTX):
        core, y = device // CTX % 2, device % SPAN
        other = y ^ 1 if core == 0 else (y + 1 if y % 2 == 1 else y - 1) % SPAN
        pairs.append((device, device - y + other))
    other_keys = lax.ppermute(cache, ("dp", "ctx"), pairs).reshape(-1, cache.shape[2])
    keys = cache.reshape(-1, cache.shape[2])
    *messages, branch, bias = pl.pallas_call(
        pack_kernel,
        out_shape=(
            *(
                jax.ShapeDtypeStruct((PEERS, message_rows(slots), LATENT), jnp.bfloat16)
                for slots in SLOTS
            ),
            jax.ShapeDtypeStruct((1,), jnp.int32),
            jax.ShapeDtypeStruct((2, ROWS + 8, keys.shape[0]), jnp.float32),
        ),
        in_specs=[SMEM, SMEM, SMEM, SMEM, VMEM, VMEM],
        out_specs=(*(VMEM for _ in SLOTS), SMEM, VMEM),
        scratch_shapes=[
            pltpu.VMEM((REQS, SLOTS[-1] * HEADS, LATENT), jnp.float32),
            pltpu.VMEM((REQS, 2 * HEADS, LATENT), jnp.float32),
            pltpu.VMEM((2, ROWS, keys.shape[0]), jnp.float32),
            pltpu.SMEM((REQS,), jnp.int32),
        ],
        compiler_params=PARAMS,
    )(ctx, dp, row_request, lengths[0], selected, queries)
    branch = branch[0]
    recv = lax.switch(
        branch, [functools.partial(to_keys, index) for index in range(len(SLOTS))], *messages
    )
    recv, other_keys = lax.optimization_barrier((recv, other_keys))
    hidden = lax.switch(
        branch,
        [functools.partial(to_heads, slots) for slots in SLOTS],
        recv, bias, keys, other_keys, w_uv, row_request,
    )
    hidden = lax.all_gather(hidden, "dp", axis=0, tiled=True)
    partial_out = jnp.dot(hidden, w_out, preferred_element_type=jnp.float32)
    partial_out = partial_out.astype(jnp.bfloat16).reshape(CTX, -1, w_out.shape[1])
    parts = lax.all_to_all(partial_out, "ctx", 0, 0)
    return jnp.sum(parts.astype(jnp.float32), axis=0).astype(jnp.bfloat16)


def solution(mesh):
    in_specs = (
        P("dp", "ctx", None),
        P("dp", "ctx", None, None),
        P("ctx", None, None),
        P("ctx", "dp"),
        P("dp", None),
        P("dp"),
        P("dp", None),
    )
    out_specs = P("ctx", "dp")
    return jax.shard_map(
        on_device, mesh=mesh, in_specs=in_specs, out_specs=out_specs, check_vma=False
    )
```
